128 devices in a mesh: loop: 16 (over x_lo, z, core), group: 8 (over y, x_hi).
Axes of the slice: x: 4 (x_hi: 2, x_lo: 2; x = x_hi * 2 + x_lo), y: 4, z: 4, core: 2. Of those that a mesh axis runs over, the one named last changes fastest.
Arguments:
- projections: float32 [32768, 256], P(('loop', 'group')), may hold values from -3 to 3
- partners: int32 [32768], P(('loop', 'group')), may hold values from 0 to 32767, as said below
Outputs:
- view_loss: float32 [32768], P(('loop', 'group'))
- gradient: float32 [32768, 256], P(('loop', 'group'))
The draws below stay inside these ranges and needn't reach their ends.
Inputs may be any that keep to these rules, and one draw needn't show every extreme that they name: partners[partners[i]] == i and partners[i] != i for every view: the views form 32768 / 2 disjoint pairs.
All inputs are finite; a program needn't handle non-finite values.
Results may differ from the reference program's by a relative error of at most 0.005.
Values may be sent and summed in bfloat16 or wider, within the bound.
A program may use at most 128 MiB of HBM per device.

```python
import jax
import jax.numpy as jnp
from jax import lax

PROJ = 256
VIEW_DEV = 256
VIEWS = 32768


def pairing(key):
    key = jax.random.fold_in(key, 5)
    return jax.random.permutation(key, VIEWS).astype(jnp.int32)


def draw_partners(key, part):
    shuffled = pairing(key)
    first_half = shuffled[0::2]
    second_half = shuffled[1::2]
    partner_ids = jnp.zeros((VIEWS,), jnp.int32).at[first_half].set(second_half).at[second_half].set(first_half)
    return partner_ids


def draw_projections(key, part):
    shuffled = pairing(key)
    key = jax.random.fold_in(key, 11)
    key_centre, key_tight, key_pair, key_jitter, key_common, key_share = jax.random.split(key, 6)
    position = jnp.zeros((VIEWS,), jnp.int32).at[shuffled].set(jnp.arange(VIEWS, dtype=jnp.int32))
    pair_of = position // 2
    cluster_of = position // 32
    clusters = (VIEWS + 31) // 32
    centres = jnp.clip(jax.random.normal(key_centre, (clusters, PROJ), jnp.float32), -4.0, 4.0)
    common = jnp.clip(jax.random.normal(key_common, (PROJ,), jnp.float32), -4.0, 4.0)
    tightness = jax.random.uniform(key_tight, (VIEWS // 2,), jnp.float32, 0.05, 0.7)
    share = jax.random.uniform(key_share, (VIEWS,), jnp.float32, 0.0, 0.36)
    pair_bases = jnp.clip(jax.random.normal(key_pair, (VIEWS // 2, PROJ), jnp.float32), -4.0, 4.0)
    jitter = jnp.clip(jax.random.normal(key_jitter, (VIEWS, PROJ), jnp.float32), -4.0, 4.0)
    pair_tight = tightness[pair_of][:, None]
    own_part = jnp.sqrt(pair_tight) * centres[cluster_of] + jnp.sqrt(0.85 - pair_tight) * pair_bases[pair_of] + 0.3873 * jitter
    view_rows = jnp.sqrt(share)[:, None] * common[None, :] + jnp.sqrt(1.0 - share)[:, None] * own_part
    return jnp.clip(view_rows, -3.0, 3.0)


def setup_inputs(seed: int = 0) -> dict:
    streams_of = jax.random.split(jax.random.key(seed), 3)
    projections = draw_projections(jax.random.fold_in(streams_of[2], 71), 0)
    partners = draw_partners(jax.random.fold_in(streams_of[2], 71), 0)
    return dict(projections=projections, partners=partners)


epsilon = 1e-06
inverse_temp = 10.0
score_bound = 10.0

def reference(projections, partners):
    inv_norm = lax.rsqrt(lax.optimization_barrier(jnp.sum(projections * projections, axis=1)) + epsilon)
    unit_rows = projections * inv_norm[:, None]
    unit_low = unit_rows.astype(jnp.bfloat16)
    widened = unit_low.astype(jnp.float32)
    columns = jnp.arange(VIEWS, dtype=jnp.int32)
    num_blocks = VIEWS // VIEW_DEV
    block_ids = jnp.arange(num_blocks, dtype=jnp.int32)

    def tile_terms(block_id):
        first_row = (block_id * VIEW_DEV).astype(jnp.int32)
        row_block = lax.dynamic_slice_in_dim(widened, first_row, VIEW_DEV, 0)
        row_index = first_row + jnp.arange(VIEW_DEV, dtype=jnp.int32)
        partner_ids = lax.dynamic_slice_in_dim(partners, first_row, VIEW_DEV, 0)
        logits = jnp.dot(row_block, widened.T, precision=lax.Precision.HIGHEST) * inverse_temp
        tile_exp = jnp.where(columns[None, :] == row_index[:, None], jnp.float32(0.0), jnp.exp(logits - score_bound))
        paired = columns[None, :] == partner_ids[:, None]
        return (logits, tile_exp, paired)

    def forward_block(block_id):
        logits, tile_exp, paired = tile_terms(block_id)
        return (lax.optimization_barrier(jnp.sum(tile_exp, axis=1)), lax.optimization_barrier(jnp.sum(jnp.where(paired, logits, jnp.float32(0.0)), axis=1)))
    row_sums, positive = lax.map(forward_block, block_ids)
    row_sums = row_sums.reshape(VIEWS)
    positive = positive.reshape(VIEWS)
    view_loss = jnp.log(row_sums) + score_bound - positive
    recip = 1.0 / row_sums

    def backward_block(block_id):
        logits, tile_exp, paired = tile_terms(block_id)
        first_row = (block_id * VIEW_DEV).astype(jnp.int32)
        recip_rows = lax.dynamic_slice_in_dim(recip, first_row, VIEW_DEV, 0)
        weights = tile_exp * (recip_rows[:, None] + recip[None, :]) - 2.0 * paired.astype(jnp.float32)
        weights = lax.optimization_barrier(weights.astype(jnp.bfloat16)).astype(jnp.float32)
        return jnp.dot(weights, widened, precision=lax.Precision.HIGHEST) * inverse_temp
    grad_unit = lax.map(backward_block, block_ids).reshape(VIEWS, PROJ)
    along = lax.optimization_barrier(jnp.sum(unit_rows * grad_unit, axis=1, keepdims=True))
    gradient = inv_norm[:, None] * (grad_unit - unit_rows * along)
    return (view_loss, gradient)
```

```python
import jax
import jax.numpy as jnp
from jax import lax
from jax.experimental import pallas as pl
from jax.experimental.pallas import tpu as pltpu
from jax.sharding import PartitionSpec as P

MESH = pl.DeviceIdType.MESH
F32, BF16 = jnp.float32, jnp.bfloat16
epsilon = 1e-06
inverse_temp = 10.0
LOG2E = 1.4426950408889634

PROJ = 256
BLK = 256
RING = 4
PLANE = 2 * RING * RING
COLS = PLANE * BLK
ROWS = RING * BLK

ORDER = [
    (0, 0), (1, 0), (3, 0), (0, 1), (0, 3), (1, 1), (3, 1), (1, 3),
    (3, 3), (2, 0), (0, 2), (2, 1), (2, 3), (1, 2), (3, 2), (2, 2),
]
STEP = {d: s for s, d in enumerate(ORDER)}


def own_pos(s):
    return 0 if s == 0 else 2 * s - 1


def sib_pos(s):
    return 2 * s + 2 if s < 15 else 31


def forwards(d):
    dx, dz = d
    out = []
    if d == (0, 0):
        return [(0, 2, (1, 0), (1, 0)), (0, 2, (3, 0), (-1, 0)), (0, 2, (0, 1), (0, 1)), (0, 2, (0, 3), (0, -1))]
    for half in (0, 1):
        a, b = (dx, dz) if half == 0 else (dz, dx)

        def there(a, b):
            return (a, b) if half == 0 else (b, a)

        first = 1 if half == 0 else 3
        if b == 0:
            if a == first:
                out.append((half, 1, there(2, 0), there(1 if first == 1 else -1, 0)))
            out.append((half, 1, there(a, 1), there(0, 1)))
            out.append((half, 1, there(a, 3), there(0, -1)))
        else:
            turn = 1 if a in (0, 1) else 3
            if b == turn:
                out.append((half, 1, there(a, 2), there(0, 1 if turn == 1 else -1)))
    return out


LEAD = 5
COMM_BEFORE = [[] for _ in range(16)]
for _s in range(LEAD, 16):
    COMM_BEFORE[min(_s - LEAD, _s - 1)].append(_s)


def transposed_sum(v):
    parts = [jnp.sum(jnp.transpose(v[i * 128 : (i + 1) * 128, :]), axis=0, keepdims=True) for i in range(2)]
    return jnp.concatenate(parts, axis=1)


def kernel(
    proj_ref, part_ref, loss_ref, grad_ref,
    u, u32, rows, e, acc, inv, enc, enc_s, pick,
    rs_send, rs_recv, r_cols, r_rows, ri, pos_send, pos_recv, g_acc, g_own, g_send, g_recv,
    own_sem, sib_sem, row_sem, enc_sem, rs_sem, rcol_sem, rrow_sem, pos_sem, g_sem, send_sem, local_sem,
):
    loop, group = lax.axis_index("loop"), lax.axis_index("group")
    core, z, x_lo = lax.rem(loop, 2), lax.rem(loop // 2, 4), loop // 8
    y, x_hi = group // 2, lax.rem(group, 2)
    x = x_hi * 2 + x_lo

    def dev(dx=0, dz=0, dy=0, dc=0):
        xx, zz, yy = lax.rem(x + dx + 4, 4), lax.rem(z + dz + 4, 4), lax.rem(y + dy + 4, 4)
        cc = 1 - core if dc else core
        return ((lax.rem(xx, 2) * 4 + zz) * 2 + cc, yy * 2 + xx // 2)

    n_send = [0]
    sent = []

    def remote(src, dst, recv, to):
        index = n_send[0]
        n_send[0] += 1

        def make():
            return pltpu.make_async_remote_copy(
                src_ref=src, dst_ref=dst, send_sem=send_sem.at[index], recv_sem=recv, device_id=to, device_id_type=MESH
            )

        sent.append(make)
        return make

    plane = [(dx, dz, dc) for dc in (0, 1) for dx in range(4) for dz in range(4) if (dx, dz, dc) != (0, 0, 0)]
    barrier = pltpu.get_barrier_semaphore()
    for dx, dz, dc in plane:
        pl.semaphore_signal(barrier, inc=1, device_id=dev(dx, dz, 0, dc), device_id_type=MESH)
    for k in (1, 2, 3):
        pl.semaphore_signal(barrier, inc=1, device_id=dev(dy=k), device_id_type=MESH)

    proj = proj_ref[...]
    inv_norm = lax.rsqrt(jnp.sum(proj * proj, axis=1, keepdims=True) + epsilon)
    inv[...] = jnp.broadcast_to(inv_norm, inv.shape)
    low = (proj * inv_norm).astype(BF16)
    u[0] = low
    rows[0] = low

    p = part_ref[...]
    off, blk = p & 255, p >> 8
    p_group, p_loop = blk & 7, blk >> 3
    p_x = ((p_group & 1) << 1) + (p_loop >> 3)
    p_z, p_c = (p_loop >> 1) & 3, p_loop & 1
    key = (p_c ^ core) * 16 + ((x - p_x) & 3) * 4 + ((z - p_z) & 3)
    place = jnp.zeros_like(p)
    for dx in range(4):
        for dz in range(4):
            s = STEP[(dx, dz)]
            place = jnp.where(key == dx * 4 + dz, own_pos(s), place)
            place = jnp.where(key == 16 + dx * 4 + dz, sib_pos(s), place)
    enc[0] = (p_group >> 1) * COLS + place * BLK + off
    u32[COLS : COLS + 8, :] = jnp.zeros((8, PROJ), F32)
    acc[...] = jnp.zeros_like(acc)

    pl.semaphore_wait(barrier, len(plane) + 3)

    row_copies = []
    for k in (2, 1, 3):
        row_copies.append(remote(u.at[0], rows.at[k], row_sem.at[k - 1], dev(dy=k)))
    enc_copies = [remote(enc.at[0], enc.at[k], enc_sem.at[k - 1], dev(dy=k)) for k in (1, 2, 3)]

    def piece(pos, half, halves):
        return u.at[pos, pl.ds(half * 128, halves * 128), :]

    comm = []
    for s, d in enumerate(ORDER):
        out = []
        for half, halves, there, (ddx, ddz) in forwards(d):
            t = STEP[there]
            out.append(
                remote(piece(own_pos(s), half, halves), piece(own_pos(t), half, halves), own_sem.at[t, half], dev(ddx, ddz))
            )
        out.append(remote(u.at[own_pos(s)], u.at[sib_pos(s)], sib_sem.at[s], dev(dc=1)))
        comm.append(out)

    def wait_for(ref, sem):
        pltpu.make_async_copy(ref, ref, sem).wait()

    def comm_step(s):
        if s in (1, 2, 3, 4):
            wait_for(u.at[own_pos(s)], own_sem.at[s, 0])
        elif s > 0:
            for half in (0, 1):
                wait_for(piece(own_pos(s), half, 1), own_sem.at[s, half])
        for make in comm[s]:
            make().start()

    comm_step(0)
    for make in row_copies + enc_copies:
        make().start()
    for s in range(1, LEAD):
        comm_step(s)
    for k in (1, 2, 3):
        wait_for(rows.at[k], row_sem.at[k - 1])

    scale = inverse_temp * LOG2E
    r_iota = lax.broadcasted_iota(jnp.int32, (BLK, BLK), 0)
    c_iota = lax.broadcasted_iota(jnp.int32, (BLK, BLK), 1)

    def compute(i, carry):
        for t in range(16):
            if COMM_BEFORE[t]:

                @pl.when(i == t)
                def _():
                    for s in COMM_BEFORE[t]:
                        comm_step(s)

        @pl.when(i >= 1)
        def _():
            wait_for(u.at[2 * i], sib_sem.at[i - 1])

        @pl.when(i == 15)
        def _():
            wait_for(u.at[31], sib_sem.at[15])

        for b in (0, 1):
            pos = 2 * i + b
            block = u[pos]
            u32[pl.ds(pl.multiple_of(pos * BLK, BLK), BLK), :] = block.astype(F32)
            for k in range(RING):
                dots = lax.dot_general(rows[k], block, (((1,), (1,)), ((), ())), preferred_element_type=F32)
                ex = jnp.exp2(dots * scale)
                if k == 0 and b == 0:
                    ex = jnp.where(r_iota == c_iota + i * BLK, 0.0, ex)
                acc[k] += ex[:, :128] + ex[:, 128:]
                e[k, pos] = ex.astype(BF16)
        return carry

    lax.fori_loop(0, 16, compute, 0)

    for k in range(RING):
        rs_send[k] = transposed_sum(acc[k])
    rs_copies = [remote(rs_send.at[k], rs_recv.at[k], rs_sem.at[k - 1], dev(dy=-k)) for k in (2, 1, 3)]
    for make in rs_copies:
        make().start()
    for k in (1, 2, 3):
        wait_for(enc.at[k], enc_sem.at[k - 1])
    to_smem = pltpu.make_async_copy(enc, enc_s, local_sem)
    to_smem.start()
    to_smem.wait()
    for k in (1, 2, 3):
        wait_for(rs_recv.at[k], rs_sem.at[k - 1])
    row_sums = rs_send[0] + rs_recv[1] + rs_recv[2] + rs_recv[3]
    recip = 1.0 / row_sums
    r_cols[0] = recip
    r_rows[0] = recip
    r_copies = []
    for dx, dz, dc in plane:
        s = STEP[(dx, dz)]
        pos = sib_pos(s) if dc else own_pos(s)
        r_copies.append(remote(r_cols.at[0], r_cols.at[pos], rcol_sem.at[pos], dev(dx, dz, 0, dc)))
    for k in (1, 2, 3):
        r_copies.append(remote(r_cols.at[0], r_rows.at[k], rrow_sem.at[k - 1], dev(dy=k)))
    for make in r_copies:
        make().start()

    for k in range(RING):

        def fetch(j, carry):
            for t in range(8):
                i = j * 8 + t
                v = enc_s[k, 0, i]
                at = jnp.where(v // COLS == y, lax.rem(v, COLS), COLS)
                pick[k, pl.ds(i, 1), :] = u32[pl.ds(at, 1), :]
            return carry

        lax.fori_loop(0, BLK // 8, fetch, 0)
    for k in range(RING):
        q = rows[k].astype(F32) * pick[k]
        pos_send[k] = transposed_sum(q[:, :128] + q[:, 128:]) * inverse_temp
    pos_copies = [remote(pos_send.at[k], pos_recv.at[k], pos_sem.at[k - 1], dev(dy=-k)) for k in (1, 2, 3)]
    for make in pos_copies:
        make().start()

    for k in (1, 2, 3):
        wait_for(r_rows.at[k], rrow_sem.at[k - 1])
    for dx, dz, dc in plane:
        s = STEP[(dx, dz)]
        pos = sib_pos(s) if dc else own_pos(s)
        wait_for(r_cols.at[pos], rcol_sem.at[pos])
    for k in range(RING):
        r = r_rows[k]
        for h in (0, 1):
            part = jnp.broadcast_to(r[:, h * 128 : (h + 1) * 128], (128, 128))
            ri[k, h * 128 : (h + 1) * 128, :] = jnp.transpose(part)

    g_copies = {k: remote(g_send.at[k], g_recv.at[k], g_sem.at[k - 1], dev(dy=-k)) for k in (1, 2, 3)}
    for k in (2, 1, 3, 0):
        g_acc[...] = jnp.zeros_like(g_acc)

        def weigh(i, carry):
            total = g_acc[...]
            r_row = jnp.concatenate([ri[k], ri[k]], axis=1)
            for b in range(4):
                pos = 4 * i + b
                w = e[k, pos].astype(F32) * (r_row + r_cols[pos])
                total += jnp.dot(w.astype(BF16), u[pos], preferred_element_type=F32)
            g_acc[...] = total
            return carry

        lax.fori_loop(0, PLANE // 4, weigh, 0)
        g = inverse_temp * (g_acc[...] - 2.0 * pick[k])
        if k:
            g_send[k] = g.astype(BF16)
            g_copies[k]().start()
        else:
            g_own[...] = g

    for k in (1, 2, 3):
        wait_for(pos_recv.at[k], pos_sem.at[k - 1])
    positive = pos_send[0] + pos_recv[1] + pos_recv[2] + pos_recv[3]
    loss_ref[...] = jnp.log(row_sums) - positive
    for k in (1, 2, 3):
        wait_for(g_recv.at[k], g_sem.at[k - 1])
    grad_unit = g_own[...] + g_recv[1].astype(F32) + g_recv[2].astype(F32) + g_recv[3].astype(F32)
    inv_b = jnp.concatenate([inv[...], inv[...]], axis=1)
    unit = proj_ref[...] * inv_b
    along = jnp.sum(unit * grad_unit, axis=1, keepdims=True)
    grad_ref[...] = inv_b * (grad_unit - unit * along)

    for make in sent:
        make().wait_send()


N_SEND = 150


def on_device(projections, partners):
    dma = pltpu.SemaphoreType.DMA
    vmem = pl.BlockSpec(memory_space=pltpu.VMEM)
    loss, grad = pl.pallas_call(
        kernel,
        out_shape=(jax.ShapeDtypeStruct((1, BLK), F32), jax.ShapeDtypeStruct((BLK, PROJ), F32)),
        in_specs=[vmem, vmem],
        out_specs=(vmem, vmem),
        scratch_shapes=[
            pltpu.VMEM((PLANE, BLK, PROJ), BF16),
            pltpu.VMEM((COLS + 8, PROJ), F32),
            pltpu.VMEM((RING, BLK, PROJ), BF16),
            pltpu.VMEM((RING, PLANE, BLK, BLK), BF16),
            pltpu.VMEM((RING, BLK, 128), F32),
            pltpu.VMEM((BLK, 128), F32),
            pltpu.VMEM((RING, 1, BLK), jnp.int32),
            pltpu.SMEM((RING, 1, BLK), jnp.int32),
            pltpu.VMEM((RING, BLK, PROJ), F32),
            pltpu.VMEM((RING, 1, BLK), F32),
            pltpu.VMEM((RING, 1, BLK), F32),
            pltpu.VMEM((PLANE, 1, BLK), F32),
            pltpu.VMEM((RING, 1, BLK), F32),
            pltpu.VMEM((RING, BLK, 128), F32),
            pltpu.VMEM((RING, 1, BLK), F32),
            pltpu.VMEM((RING, 1, BLK), F32),
            pltpu.VMEM((BLK, PROJ), F32),
            pltpu.VMEM((BLK, PROJ), F32),
            pltpu.VMEM((RING, BLK, PROJ), BF16),
            pltpu.VMEM((RING, BLK, PROJ), BF16),
            dma((16, 2)), dma((16,)), dma((3,)), dma((3,)), dma((3,)), dma((PLANE,)), dma((3,)), dma((3,)), dma((3,)),
            dma((N_SEND,)), dma,
        ],
        compiler_params=pltpu.CompilerParams(
            collective_id=0, has_side_effects=True, vmem_limit_bytes=48 * 1024 * 1024
        ),
        cost_estimate=pl.CostEstimate(flops=4 * ROWS * COLS * PROJ, bytes_accessed=8 << 20, transcendentals=ROWS * COLS),
    )(projections, partners.reshape(1, BLK))
    return loss.reshape(BLK), grad


def solution(mesh):
    return jax.shard_map(
        on_device,
        mesh=mesh,
        in_specs=(P(("loop", "group"), None), P(("loop", "group"))),
        out_specs=(P(("loop", "group")), P(("loop", "group"), None)),
        check_vma=False,
    )
```

```python
import jax
import jax.numpy as jnp
from jax import lax
from jax.experimental import pallas as pl
from jax.experimental.pallas import tpu as pltpu
from jax.sharding import PartitionSpec as P

MESH = pl.DeviceIdType.MESH
F32, BF16 = jnp.float32, jnp.bfloat16
epsilon = 1e-06
inverse_temp = 10.0
LOG2E = 1.4426950408889634

PROJ = 256
BLK = 256
RING = 4
PLANE = 2 * RING * RING
COLS = PLANE * BLK
ROWS = RING * BLK

ORDER = [
    (0, 0), (1, 0), (3, 0), (0, 1), (0, 3), (2, 0), (0, 2), (1, 1),
    (3, 1), (1, 3), (3, 3), (1, 2), (3, 2), (2, 1), (2, 3), (2, 2),
]
STEP = {d: s for s, d in enumerate(ORDER)}
DY = (2, 1, 3, 0)
SLOT = {dy: k for k, dy in enumerate(DY)}
OWN = SLOT[0]


def own_pos(s):
    return 0 if s == 0 else 2 * s - 1


def sib_pos(s):
    return 2 * s + 2 if s < 15 else 31


def transposed_sum(v):
    parts = [jnp.sum(jnp.transpose(v[i * 128 : (i + 1) * 128, :]), axis=0, keepdims=True) for i in range(2)]
    return jnp.concatenate(parts, axis=1)


def kernel(
    proj_hbm, part_hbm, loss_ref, grad_ref,
    proj_ref, part_ref, u, u32, rows, e, acc, inv, enc, enc_s, pick,
    rs_send, rs_recv, r_cols, r_rows, ri, pos_send, pos_recv, g_own, g_send, g_recv,
    own_sem, sib_sem, row_sem, enc_sem, rs_sem, rcol_sem, rrow_sem, pos_sem, g_sem, send_sem, local_sem, in_sem,
):
    loop, group = lax.axis_index("loop"), lax.axis_index("group")
    core, z, x_lo = lax.rem(loop, 2), lax.rem(loop // 2, 4), loop // 8
    y, x_hi = group // 2, lax.rem(group, 2)
    x = x_hi * 2 + x_lo

    def dev(dx=0, dz=0, dy=0, dc=0):
        xx, zz, yy = lax.rem(x + dx + 4, 4), lax.rem(z + dz + 4, 4), lax.rem(y + dy + 4, 4)
        cc = 1 - core if dc else core
        return ((lax.rem(xx, 2) * 4 + zz) * 2 + cc, yy * 2 + xx // 2)

    n_send = [0]
    sent = []

    def remote(src, dst, recv, to):
        index = n_send[0]
        n_send[0] += 1

        def make():
            return pltpu.make_async_remote_copy(
                src_ref=src, dst_ref=dst, send_sem=send_sem.at[index], recv_sem=recv, device_id=to, device_id_type=MESH
            )

        sent.append(make)
        return make

    proj_in = pltpu.make_async_copy(proj_hbm, proj_ref, in_sem.at[0])
    part_in = pltpu.make_async_copy(part_hbm, part_ref, in_sem.at[1])
    proj_in.start()
    part_in.start()
    plane = [(dx, dz, dc) for dc in (0, 1) for dz in (2, 1, 3, 0) for dx in (2, 1, 3, 0) if (dx, dz, dc) != (0, 0, 0)]
    near = [dev(dx=k) for k in (1, 2, 3)] + [dev(dz=k) for k in (1, 2, 3)] + [dev(dy=k) for k in (1, 2, 3)] + [dev(dc=1)]
    barrier = pltpu.get_barrier_semaphore()
    for to in near:
        pl.semaphore_signal(barrier, inc=1, device_id=to, device_id_type=MESH)

    proj_in.wait()
    proj = proj_ref[...]
    inv_norm = lax.rsqrt(jnp.sum(proj * proj, axis=1, keepdims=True) + epsilon)
    inv[...] = jnp.broadcast_to(inv_norm, inv.shape)
    low = (proj * inv_norm).astype(BF16)
    u[0] = low
    rows[OWN] = low
    part_in.wait()

    p = part_ref[...]
    off, blk = p & 255, p >> 8
    p_group, p_loop = blk & 7, blk >> 3
    p_x = ((p_group & 1) << 1) + (p_loop >> 3)
    p_z, p_c = (p_loop >> 1) & 3, p_loop & 1
    key = (p_c ^ core) * 16 + ((x - p_x) & 3) * 4 + ((z - p_z) & 3)
    place = jnp.zeros_like(p)
    for dx in range(4):
        for dz in range(4):
            s = STEP[(dx, dz)]
            place = jnp.where(key == dx * 4 + dz, own_pos(s), place)
            place = jnp.where(key == 16 + dx * 4 + dz, sib_pos(s), place)
    enc[OWN] = (p_group >> 1) * COLS + place * BLK + off
    u32[COLS : COLS + 8, :] = jnp.zeros((8, PROJ), F32)
    acc[...] = jnp.zeros_like(acc)

    pl.semaphore_wait(barrier, len(near))

    def wait_for(ref, sem):
        pltpu.make_async_copy(ref, ref, sem).wait()

    line = [(k, DY[k]) for k in range(RING) if DY[k]]
    row_copies = [remote(u.at[0], rows.at[k], row_sem.at[k], dev(dy=dy)) for k, dy in line]
    enc_copies = [remote(enc.at[OWN], enc.at[k], enc_sem.at[k], dev(dy=dy)) for k, dy in line]

    def piece(s, half):
        return u.at[own_pos(s), pl.ds(half * 128, 128), :]

    def along(half, d):
        return (d, 0) if half == 0 else (0, d)

    def push(s, half, axis, d):
        dx, dz = ORDER[s]
        t = STEP[((dx + d) % 4, dz) if axis == 0 else (dx, (dz + d) % 4)]
        remote(piece(s, half), piece(t, half), own_sem.at[t, half], dev(dx=d) if axis == 0 else dev(dz=d))().start()

    def wait_half(s, half):
        wait_for(piece(s, half), own_sem.at[s, half])

    sib_copies = [remote(u.at[own_pos(s)], u.at[sib_pos(s)], sib_sem.at[s], dev(dc=1)) for s in range(16)]

    for half in (0, 1):
        for d in (1, 3, 2):
            push(0, half, half, d)
    for k in (1, 2, 0):
        row_copies[k]().start()
    for half in (0, 1):
        for d in (1, 3, 2):
            push(0, half, 1 - half, d)
    sib_copies[0]().start()
    for make in enc_copies:
        make().start()
    for d in (1, 3, 2):
        for half in (0, 1):
            s = STEP[along(half, d)]
            wait_half(s, half)
            for f in (1, 3, 2):
                push(s, half, 1 - half, f)
    for s in range(1, 7):
        wait_half(s, 0 if ORDER[s][0] == 0 else 1)
        sib_copies[s]().start()
    for k, dy in line:
        wait_for(rows.at[k], row_sem.at[k])

    def comm_step(s):
        wait_half(s, 0)
        wait_half(s, 1)
        sib_copies[s]().start()

    scale = inverse_temp * LOG2E
    r_iota = lax.broadcasted_iota(jnp.int32, (BLK, BLK), 0)
    c_iota = lax.broadcasted_iota(jnp.int32, (BLK, BLK), 1)

    def compute(i, carry):
        for t in range(16):
            if 7 <= t + 1 <= 15:

                @pl.when(i == t)
                def _():
                    comm_step(t + 1)

        @pl.when(i >= 1)
        def _():
            wait_for(u.at[2 * i], sib_sem.at[i - 1])

        @pl.when(i == 15)
        def _():
            wait_for(u.at[31], sib_sem.at[15])

        for b in (0, 1):
            pos = 2 * i + b
            block = u[pos]
            u32[pl.ds(pl.multiple_of(pos * BLK, BLK), BLK), :] = block.astype(F32)
            for k in range(RING):
                dots = lax.dot_general(rows[k], block, (((1,), (1,)), ((), ())), preferred_element_type=F32)
                ex = jnp.exp2(dots * scale)
                if k == OWN and b == 0:
                    ex = jnp.where(r_iota == c_iota + i * BLK, 0.0, ex)
                acc[k] += ex[:, :128] + ex[:, 128:]
                e[k, pos] = ex.astype(BF16)
        return carry

    lax.fori_loop(0, 16, compute, 0)

    for k in range(RING):
        rs_send[k] = transposed_sum(acc[k])
    rs_copies = [remote(rs_send.at[k], rs_recv.at[k], rs_sem.at[k], dev(dy=-dy)) for k, dy in line]
    for make in rs_copies:
        make().start()
    for k, dy in line:
        wait_for(enc.at[k], enc_sem.at[k])
    to_smem = pltpu.make_async_copy(enc, enc_s, local_sem)
    to_smem.start()
    to_smem.wait()
    for k, dy in line:
        wait_for(rs_recv.at[k], rs_sem.at[k])
    row_sums = rs_send[OWN] + rs_recv[0] + rs_recv[1] + rs_recv[2]
    recip = 1.0 / row_sums
    r_cols[0] = recip
    r_rows[OWN] = recip
    r_copies = []
    for dx, dz, dc in plane:
        s = STEP[(dx, dz)]
        pos = sib_pos(s) if dc else own_pos(s)
        r_copies.append(remote(r_cols.at[0], r_cols.at[pos], rcol_sem.at[pos], dev(dx, dz, 0, dc)))
    for k, dy in line:
        r_copies.append(remote(r_cols.at[0], r_rows.at[k], rrow_sem.at[k], dev(dy=dy)))
    for make in r_copies:
        make().start()

    for k in range(RING):

        def fetch(j, carry):
            for t in range(8):
                i = j * 8 + t
                v = enc_s[k, 0, i]
                at = jnp.where(v // COLS == y, lax.rem(v, COLS), COLS)
                pick[k, pl.ds(i, 1), :] = u32[pl.ds(at, 1), :]
            return carry

        lax.fori_loop(0, BLK // 8, fetch, 0)
    for k in range(RING):
        q = rows[k].astype(F32) * pick[k]
        pos_send[k] = transposed_sum(q[:, :128] + q[:, 128:]) * inverse_temp
    pos_copies = [remote(pos_send.at[k], pos_recv.at[k], pos_sem.at[k], dev(dy=-dy)) for k, dy in line]
    for make in pos_copies:
        make().start()

    for k, dy in line:
        wait_for(r_rows.at[k], rrow_sem.at[k])
    for dx, dz, dc in plane:
        s = STEP[(dx, dz)]
        pos = sib_pos(s) if dc else own_pos(s)
        wait_for(r_cols.at[pos], rcol_sem.at[pos])
    for k in range(RING):
        r = r_rows[k]
        for h in (0, 1):
            part = jnp.broadcast_to(r[:, h * 128 : (h + 1) * 128], (128, 128))
            ri[k, h * 128 : (h + 1) * 128, :] = jnp.transpose(part)

    g_copies = [remote(g_send.at[k], g_recv.at[k], g_sem.at[k], dev(dy=-dy)) for k, dy in line]

    def weigh(k, carry):
        r_row = jnp.concatenate([ri[k], ri[k]], axis=1)
        total = jnp.zeros((BLK, PROJ), F32)
        for pos in range(PLANE):
            w = e[k, pos].astype(F32) * (r_row + r_cols[pos])
            total += jnp.dot(w.astype(BF16), u[pos], preferred_element_type=F32)
        g = inverse_temp * (total - 2.0 * pick[k])
        g_own[...] = g
        g_send[k] = g.astype(BF16)
        for t in range(3):

            @pl.when(k == t)
            def _():
                g_copies[t]().start()

        return carry

    lax.fori_loop(0, RING, weigh, 0)

    for k, dy in line:
        wait_for(pos_recv.at[k], pos_sem.at[k])
    positive = pos_send[OWN] + pos_recv[0] + pos_recv[1] + pos_recv[2]
    loss_ref[...] = jnp.log(row_sums) - positive
    for k, dy in line:
        wait_for(g_recv.at[k], g_sem.at[k])
    grad_unit = g_own[...] + g_recv[0].astype(F32) + g_recv[1].astype(F32) + g_recv[2].astype(F32)
    inv_b = jnp.concatenate([inv[...], inv[...]], axis=1)
    unit = proj_ref[...] * inv_b
    along = jnp.sum(unit * grad_unit, axis=1, keepdims=True)
    grad_ref[...] = inv_b * (grad_unit - unit * along)

    for make in sent:
        make().wait_send()


N_SEND = 150


def on_device(projections, partners):
    dma = pltpu.SemaphoreType.DMA
    vmem = pl.BlockSpec(memory_space=pltpu.VMEM)
    loss, grad = pl.pallas_call(
        kernel,
        out_shape=(jax.ShapeDtypeStruct((1, BLK), F32), jax.ShapeDtypeStruct((BLK, PROJ), F32)),
        in_specs=[pl.BlockSpec(memory_space=pltpu.HBM)] * 2,
        out_specs=(vmem, vmem),
        scratch_shapes=[
            pltpu.VMEM((BLK, PROJ), F32),
            pltpu.VMEM((1, BLK), jnp.int32),
            pltpu.VMEM((PLANE, BLK, PROJ), BF16),
            pltpu.VMEM((COLS + 8, PROJ), F32),
            pltpu.VMEM((RING, BLK, PROJ), BF16),
            pltpu.VMEM((RING, PLANE, BLK, BLK), BF16),
            pltpu.VMEM((RING, BLK, 128), F32),
            pltpu.VMEM((BLK, 128), F32),
            pltpu.VMEM((RING, 1, BLK), jnp.int32),
            pltpu.SMEM((RING, 1, BLK), jnp.int32),
            pltpu.VMEM((RING, BLK, PROJ), F32),
            pltpu.VMEM((RING, 1, BLK), F32),
            pltpu.VMEM((RING, 1, BLK), F32),
            pltpu.VMEM((PLANE, 1, BLK), F32),
            pltpu.VMEM((RING, 1, BLK), F32),
            pltpu.VMEM((RING, BLK, 128), F32),
            pltpu.VMEM((RING, 1, BLK), F32),
            pltpu.VMEM((RING, 1, BLK), F32),
            pltpu.VMEM((BLK, PROJ), F32),
            pltpu.VMEM((RING, BLK, PROJ), BF16),
            pltpu.VMEM((RING, BLK, PROJ), BF16),
            dma((16, 2)), dma((16,)), dma((3,)), dma((3,)), dma((3,)), dma((PLANE,)), dma((3,)), dma((3,)), dma((3,)),
            dma((N_SEND,)), dma, dma((2,)),
        ],
        compiler_params=pltpu.CompilerParams(
            collective_id=0, has_side_effects=True, vmem_limit_bytes=48 * 1024 * 1024
        ),
        cost_estimate=pl.CostEstimate(flops=4 * ROWS * COLS * PROJ, bytes_accessed=8 << 20, transcendentals=ROWS * COLS),
    )(projections, partners.reshape(1, BLK))
    return loss.reshape(BLK), grad


def solution(mesh):
    return jax.shard_map(
        on_device,
        mesh=mesh,
        in_specs=(P(("loop", "group"), None), P(("loop", "group"))),
        out_specs=(P(("loop", "group")), P(("loop", "group"), None)),
        check_vma=False,
    )
```

```python
import jax
import jax.numpy as jnp
from jax import lax
from jax.experimental import pallas as pl
from jax.experimental.pallas import tpu as pltpu
from jax.sharding import PartitionSpec as P

MESH = pl.DeviceIdType.MESH
F32, BF16 = jnp.float32, jnp.bfloat16
epsilon = 1e-06
inverse_temp = 10.0
LOG2E = 1.4426950408889634

PROJ = 256
BLK = 256
RING = 4
PLANE = 2 * RING * RING
COLS = PLANE * BLK
ROWS = RING * BLK

ORDER = [
    (0, 0), (1, 0), (3, 0), (0, 1), (0, 3), (2, 0), (0, 2), (1, 1),
    (3, 1), (1, 3), (3, 3), (1, 2), (3, 2), (2, 1), (2, 3), (2, 2),
]
STEP = {d: s for s, d in enumerate(ORDER)}
DY = (2, 1, 3, 0)
SLOT = {dy: k for k, dy in enumerate(DY)}
OWN = SLOT[0]
S_PLANE, S_ROW, S_ENC, S_RS, S_RCOL, S_RROW, S_POS, S_G = range(8)


def own_pos(s):
    return 0 if s == 0 else 2 * s - 1


def sib_pos(s):
    return 2 * s + 2 if s < 15 else 31


def transposed_sum(v):
    parts = [jnp.sum(jnp.transpose(v[i * 128 : (i + 1) * 128, :]), axis=0, keepdims=True) for i in range(2)]
    return jnp.concatenate(parts, axis=1)


def kernel(
    proj_hbm, part_hbm, loss_ref, grad_ref,
    proj_ref, part_ref, u, u32, rows, e, acc, inv, enc, index, index_s, pick,
    rs_send, rs_recv, r_cols, r_rows, ri, pos_send, pos_recv, g_own, g_send, g_recv,
    own_sem, sib_sem, row_sem, enc_sem, rs_sem, rcol_sem, rrow_sem, pos_sem, g_sem, send_sem, local_sem, in_sem,
):
    loop, group = lax.axis_index("loop"), lax.axis_index("group")
    core, z, x_lo = lax.rem(loop, 2), lax.rem(loop // 2, 4), loop // 8
    y, x_hi = group // 2, lax.rem(group, 2)
    x = x_hi * 2 + x_lo

    def dev(dx=0, dz=0, dy=0, dc=0):
        xx, zz, yy = lax.rem(x + dx + 4, 4), lax.rem(z + dz + 4, 4), lax.rem(y + dy + 4, 4)
        cc = 1 - core if dc else core
        return ((lax.rem(xx, 2) * 4 + zz) * 2 + cc, yy * 2 + xx // 2)

    def remote(src, dst, send, recv, to):
        return pltpu.make_async_remote_copy(
            src_ref=src, dst_ref=dst, send_sem=send_sem.at[send], recv_sem=recv, device_id=to, device_id_type=MESH
        )

    proj_in = pltpu.make_async_copy(proj_hbm, proj_ref, in_sem.at[0])
    part_in = pltpu.make_async_copy(part_hbm, part_ref, in_sem.at[1])
    proj_in.start()
    part_in.start()
    plane = [(dx, dz, dc) for dc in (0, 1) for dz in (2, 1, 3, 0) for dx in (2, 1, 3, 0) if (dx, dz, dc) != (0, 0, 0)]
    near = [dev(dx=k) for k in (1, 2, 3)] + [dev(dz=k) for k in (1, 2, 3)] + [dev(dy=k) for k in (1, 2, 3)] + [dev(dc=1)]
    barrier = pltpu.get_barrier_semaphore()
    for to in near:
        pl.semaphore_signal(barrier, inc=1, device_id=to, device_id_type=MESH)

    proj_in.wait()
    proj = proj_ref[...]
    inv_norm = lax.rsqrt(jnp.sum(proj * proj, axis=1, keepdims=True) + epsilon)
    inv[...] = jnp.broadcast_to(inv_norm, inv.shape)
    low = (proj * inv_norm).astype(BF16)
    u[0] = low
    rows[OWN] = low
    part_in.wait()

    p = part_ref[...].reshape(1, BLK)
    off, blk = p & 255, p >> 8
    p_group, p_loop = blk & 7, blk >> 3
    p_x = ((p_group & 1) << 1) + (p_loop >> 3)
    p_z, p_c = (p_loop >> 1) & 3, p_loop & 1
    key = (p_c ^ core) * 16 + ((x - p_x) & 3) * 4 + ((z - p_z) & 3)
    place = jnp.zeros_like(p)
    for dx in range(4):
        for dz in range(4):
            s = STEP[(dx, dz)]
            place = jnp.where(key == dx * 4 + dz, own_pos(s), place)
            place = jnp.where(key == 16 + dx * 4 + dz, sib_pos(s), place)
    enc[OWN] = (p_group >> 1) * COLS + place * BLK + off
    u32[COLS : COLS + 8, :] = jnp.zeros((8, PROJ), F32)
    acc[...] = jnp.zeros_like(acc)

    pl.semaphore_wait(barrier, len(near))

    def wait_for(ref, sem):
        pltpu.make_async_copy(ref, ref, sem).wait()

    line = [(k, DY[k]) for k in range(RING) if DY[k]]
    row_copies = [remote(u.at[0], rows.at[k], S_ROW, row_sem, dev(dy=dy)) for k, dy in line]
    enc_copies = [remote(enc.at[OWN], enc.at[k], S_ENC, enc_sem, dev(dy=dy)) for k, dy in line]

    def piece(s, half):
        return u.at[own_pos(s), pl.ds(half * 128, 128), :]

    def along(half, d):
        return (d, 0) if half == 0 else (0, d)

    def push(s, half, axis, d):
        dx, dz = ORDER[s]
        t = STEP[((dx + d) % 4, dz) if axis == 0 else (dx, (dz + d) % 4)]
        remote(piece(s, half), piece(t, half), S_PLANE, own_sem.at[t, half], dev(dx=d) if axis == 0 else dev(dz=d)).start()

    def wait_half(s, half):
        wait_for(piece(s, half), own_sem.at[s, half])

    sib_copies = [remote(u.at[own_pos(s)], u.at[sib_pos(s)], S_PLANE, sib_sem.at[s], dev(dc=1)) for s in range(16)]

    for half in (0, 1):
        for d in (1, 3, 2):
            push(0, half, half, d)
    for k in (1, 2, 0):
        row_copies[k].start()
    for half in (0, 1):
        for d in (1, 3, 2):
            push(0, half, 1 - half, d)
    sib_copies[0].start()
    for copy in enc_copies:
        copy.start()
    for d in (1, 3, 2):
        for half in (0, 1):
            s = STEP[along(half, d)]
            wait_half(s, half)
            for f in (1, 3, 2):
                push(s, half, 1 - half, f)
    for s in range(1, 7):
        wait_half(s, 0 if ORDER[s][0] == 0 else 1)
        sib_copies[s].start()
    wait_for(rows.at[pl.ds(0, 3)], row_sem)
    wait_for(enc.at[pl.ds(0, 3)], enc_sem)
    v = enc[...]
    index[...] = jnp.where((v >> 13) == y, v & (COLS - 1), COLS)
    to_smem = pltpu.make_async_copy(index, index_s, local_sem)
    to_smem.start()

    def comm_step(s):
        wait_half(s, 0)
        wait_half(s, 1)
        sib_copies[s].start()

    scale = inverse_temp * LOG2E
    r_iota = lax.broadcasted_iota(jnp.int32, (BLK, BLK), 0)
    c_iota = lax.broadcasted_iota(jnp.int32, (BLK, BLK), 1)

    def compute(i, carry):
        for t in range(16):
            if 7 <= t + 1 <= 15:

                @pl.when(i == t)
                def _():
                    comm_step(t + 1)

        @pl.when(i >= 1)
        def _():
            wait_for(u.at[2 * i], sib_sem.at[i - 1])

        @pl.when(i == 15)
        def _():
            wait_for(u.at[31], sib_sem.at[15])

        for b in (0, 1):
            pos = 2 * i + b
            block = u[pos]
            u32[pl.ds(pl.multiple_of(pos * BLK, BLK), BLK), :] = block.astype(F32)
            for k in range(RING):
                dots = lax.dot_general(rows[k], block, (((1,), (1,)), ((), ())), preferred_element_type=F32)
                ex = jnp.exp2(dots * scale)
                if k == OWN and b == 0:
                    ex = jnp.where(r_iota == c_iota + i * BLK, 0.0, ex)
                acc[k] += ex[:, :128] + ex[:, 128:]
                e[k, pos] = ex.astype(BF16)
        return carry

    lax.fori_loop(0, 16, compute, 0)

    for k in range(RING):
        rs_send[k] = transposed_sum(acc[k])
    rs_copies = [remote(rs_send.at[k], rs_recv.at[k], S_RS, rs_sem, dev(dy=-dy)) for k, dy in line]
    for copy in rs_copies:
        copy.start()
    to_smem.wait()
    wait_for(rs_recv.at[pl.ds(0, 3)], rs_sem)
    row_sums = rs_send[OWN] + rs_recv[0] + rs_recv[1] + rs_recv[2]
    recip = 1.0 / row_sums
    r_cols[0] = recip
    r_rows[OWN] = recip
    r_copies = []
    for dx, dz, dc in plane:
        s = STEP[(dx, dz)]
        pos = sib_pos(s) if dc else own_pos(s)
        r_copies.append(remote(r_cols.at[0], r_cols.at[pos], S_RCOL, rcol_sem, dev(dx, dz, 0, dc)))
    for k, dy in line:
        r_copies.append(remote(r_cols.at[0], r_rows.at[k], S_RROW, rrow_sem, dev(dy=dy)))
    for copy in r_copies:
        copy.start()

    for k in range(RING):

        def fetch(j, carry):
            for t in range(32):
                i = j * 32 + t
                pick[k, pl.ds(i, 1), :] = u32[pl.ds(index_s[k, 0, i], 1), :]
            return carry

        lax.fori_loop(0, BLK // 32, fetch, 0)
    for k in range(RING):
        q = rows[k].astype(F32) * pick[k]
        pos_send[k] = transposed_sum(q[:, :128] + q[:, 128:]) * inverse_temp
    pos_copies = [remote(pos_send.at[k], pos_recv.at[k], S_POS, pos_sem, dev(dy=-dy)) for k, dy in line]
    for copy in pos_copies:
        copy.start()

    wait_for(r_rows.at[pl.ds(0, 3)], rrow_sem)
    wait_for(r_cols.at[pl.ds(1, PLANE - 1)], rcol_sem)
    for k in range(RING):
        r = r_rows[k]
        for h in (0, 1):
            part = jnp.broadcast_to(r[:, h * 128 : (h + 1) * 128], (128, 128))
            ri[k, h * 128 : (h + 1) * 128, :] = jnp.transpose(part)

    g_copies = [remote(g_send.at[k], g_recv.at[k], S_G, g_sem, dev(dy=-dy)) for k, dy in line]

    def weigh(k, carry):
        r_row = jnp.concatenate([ri[k], ri[k]], axis=1)
        total = jnp.zeros((BLK, PROJ), F32)
        for pos in range(PLANE):
            w = e[k, pos].astype(F32) * (r_row + r_cols[pos])
            total += jnp.dot(w.astype(BF16), u[pos], preferred_element_type=F32)
        g = inverse_temp * (total - 2.0 * pick[k])
        g_own[...] = g
        g_send[k] = g.astype(BF16)
        for t in range(3):

            @pl.when(k == t)
            def _():
                g_copies[t].start()

        return carry

    lax.fori_loop(0, RING, weigh, 0)

    wait_for(pos_recv.at[pl.ds(0, 3)], pos_sem)
    positive = pos_send[OWN] + pos_recv[0] + pos_recv[1] + pos_recv[2]
    loss_ref[...] = (jnp.log(row_sums) - positive).reshape(BLK)
    wait_for(g_recv.at[pl.ds(0, 3)], g_sem)
    grad_unit = g_own[...] + g_recv[0].astype(F32) + g_recv[1].astype(F32) + g_recv[2].astype(F32)
    inv_b = jnp.concatenate([inv[...], inv[...]], axis=1)
    unit = proj_ref[...] * inv_b
    along = jnp.sum(unit * grad_unit, axis=1, keepdims=True)
    grad_ref[...] = inv_b * (grad_unit - unit * along)

    wait_for(u.at[pl.ds(0, 31)], send_sem.at[S_PLANE])
    for sem, ref in (
        (S_ROW, rows), (S_ENC, enc), (S_RS, rs_send), (S_RROW, r_rows), (S_POS, pos_send), (S_G, g_send),
    ):
        wait_for(ref.at[pl.ds(0, 3)], send_sem.at[sem])
    wait_for(r_cols.at[pl.ds(1, PLANE - 1)], send_sem.at[S_RCOL])


def on_device(projections, partners):
    dma = pltpu.SemaphoreType.DMA
    vmem = pl.BlockSpec(memory_space=pltpu.VMEM)
    loss, grad = pl.pallas_call(
        kernel,
        out_shape=(jax.ShapeDtypeStruct((BLK,), F32), jax.ShapeDtypeStruct((BLK, PROJ), F32)),
        in_specs=[pl.BlockSpec(memory_space=pltpu.HBM)] * 2,
        out_specs=(vmem, vmem),
        scratch_shapes=[
            pltpu.VMEM((BLK, PROJ), F32),
            pltpu.VMEM((BLK,), jnp.int32),
            pltpu.VMEM((PLANE, BLK, PROJ), BF16),
            pltpu.VMEM((COLS + 8, PROJ), F32),
            pltpu.VMEM((RING, BLK, PROJ), BF16),
            pltpu.VMEM((RING, PLANE, BLK, BLK), BF16),
            pltpu.VMEM((RING, BLK, 128), F32),
            pltpu.VMEM((BLK, 128), F32),
            pltpu.VMEM((RING, 1, BLK), jnp.int32),
            pltpu.VMEM((RING, 1, BLK), jnp.int32),
            pltpu.SMEM((RING, 1, BLK), jnp.int32),
            pltpu.VMEM((RING, BLK, PROJ), F32),
            pltpu.VMEM((RING, 1, BLK), F32),
            pltpu.VMEM((RING, 1, BLK), F32),
            pltpu.VMEM((PLANE, 1, BLK), F32),
            pltpu.VMEM((RING, 1, BLK), F32),
            pltpu.VMEM((RING, BLK, 128), F32),
            pltpu.VMEM((RING, 1, BLK), F32),
            pltpu.VMEM((RING, 1, BLK), F32),
            pltpu.VMEM((BLK, PROJ), F32),
            pltpu.VMEM((RING, BLK, PROJ), BF16),
            pltpu.VMEM((RING, BLK, PROJ), BF16),
            dma((16, 2)), dma((16,)), dma, dma, dma, dma, dma, dma, dma, dma((8,)), dma, dma((2,)),
        ],
        compiler_params=pltpu.CompilerParams(
            collective_id=0, has_side_effects=True, vmem_limit_bytes=54850 * 1024
        ),
        cost_estimate=pl.CostEstimate(flops=4 * ROWS * COLS * PROJ, bytes_accessed=8 << 20, transcendentals=ROWS * COLS),
    )(projections, partners)
    return loss, grad


def solution(mesh):
    return jax.shard_map(
        on_device,
        mesh=mesh,
        in_specs=(P(("loop", "group"), None), P(("loop", "group"))),
        out_specs=(P(("loop", "group")), P(("loop", "group"), None)),
        check_vma=False,
    )
```

```python
import jax
import jax.numpy as jnp
from jax import lax
from jax.experimental import pallas as pl
from jax.experimental.pallas import tpu as pltpu
from jax.sharding import PartitionSpec as P

MESH = pl.DeviceIdType.MESH
F32, BF16 = jnp.float32, jnp.bfloat16
epsilon = 1e-06
inverse_temp = 10.0
LOG2E = 1.4426950408889634

PROJ = 256
BLK = 256
RING = 4
PLANE = RING * RING
COLS = PLANE * BLK
LINE = 2 * RING

ORDER = [
    (0, 0), (1, 0), (0, 1), (3, 0), (0, 3), (2, 0), (0, 2), (1, 1),
    (3, 1), (1, 3), (3, 3), (1, 2), (3, 2), (2, 1), (2, 3), (2, 2),
]
STEP = {d: s for s, d in enumerate(ORDER)}
SLOTS = ((1, 2), (1, 1), (0, 2), (1, 3), (0, 1), (1, 0), (0, 3), (0, 0))
OWN = 7
TWOS = 7
FIRST = 3
LINE_DY = (2, 1, 3, 0)
S_PLANE, S_ROW, S_ENC, S_RS, S_RCOL, S_RROW, S_POS, S_G, S_SIB = range(9)


def transposed_sum(v):
    parts = [jnp.sum(jnp.transpose(v[i * 128 : (i + 1) * 128, :]), axis=0, keepdims=True) for i in range(2)]
    return jnp.concatenate(parts, axis=1)


def kernel(
    proj_hbm, part_hbm, loss_ref, grad_ref,
    proj_ref, part_ref, u, u32, rows, e, acc, inv, enc, index, index_s, pick,
    rs_send, rs_recv, r_cols, r_rows, ri, pos_send, pos_recv, g_own, g_send, g_recv, s_send, s_recv,
    own_sem, row_sem, row_sib_sem, enc_sem, rs_sem, rcol_sem, rrow_sem, pos_sem, g_sem, s_sem, send_sem, local_sem, in_sem,
):
    loop, group = lax.axis_index("loop"), lax.axis_index("group")
    core, z, x_lo = lax.rem(loop, 2), lax.rem(loop // 2, 4), loop // 8
    y, x_hi = group // 2, lax.rem(group, 2)
    x = x_hi * 2 + x_lo

    def dev(dx=0, dz=0, dy=0, dc=0):
        xx, zz, yy = lax.rem(x + dx + 4, 4), lax.rem(z + dz + 4, 4), lax.rem(y + dy + 4, 4)
        cc = 1 - core if dc else core
        return ((lax.rem(xx, 2) * 4 + zz) * 2 + cc, yy * 2 + xx // 2)

    def remote(src, dst, send, recv, to):
        return pltpu.make_async_remote_copy(
            src_ref=src, dst_ref=dst, send_sem=send_sem.at[send], recv_sem=recv, device_id=to, device_id_type=MESH
        )

    proj_in = pltpu.make_async_copy(proj_hbm, proj_ref, in_sem.at[0])
    part_in = pltpu.make_async_copy(part_hbm, part_ref, in_sem.at[1])
    proj_in.start()
    part_in.start()
    plane = [(dx, dz) for dz in (2, 1, 3, 0) for dx in (2, 1, 3, 0) if (dx, dz) != (0, 0)]
    line = [(j, dc, dy) for j, (dc, dy) in enumerate(SLOTS) if j != OWN]
    near = [dev(dx=k) for k in (1, 2, 3)] + [dev(dz=k) for k in (1, 2, 3)] + [dev(dy=k) for k in (1, 2, 3)] + [dev(dc=1)]
    barrier = pltpu.get_barrier_semaphore()
    for to in near:
        pl.semaphore_signal(barrier, inc=1, device_id=to, device_id_type=MESH)

    proj_in.wait()
    proj = proj_ref[...]
    inv_norm = lax.rsqrt(jnp.sum(proj * proj, axis=1, keepdims=True) + epsilon)
    inv[...] = jnp.broadcast_to(inv_norm, inv.shape)
    low = (proj * inv_norm).astype(BF16)
    u[0] = low
    rows[OWN] = low
    part_in.wait()

    p = part_ref[...].reshape(1, BLK)
    off, blk = p & 255, p >> 8
    p_group, p_loop = blk & 7, blk >> 3
    p_x = ((p_group & 1) << 1) + (p_loop >> 3)
    p_z, p_c = (p_loop >> 1) & 3, p_loop & 1
    key = ((x - p_x) & 3) * 4 + ((z - p_z) & 3)
    place = jnp.zeros_like(p)
    for d, t in STEP.items():
        place = jnp.where(key == d[0] * 4 + d[1], t, place)
    enc[OWN] = ((p_group >> 1) * 2 + p_c) * COLS + place * BLK + off
    u32[COLS : COLS + 8, :] = jnp.zeros((8, PROJ), F32)
    acc[...] = jnp.zeros_like(acc)

    pl.semaphore_wait(barrier, len(near))

    def wait_for(ref, sem):
        pltpu.make_async_copy(ref, ref, sem).wait()

    def row_copy(dy):
        t = SLOTS.index((0, dy))
        return remote(u.at[0], rows.at[t], S_ROW, row_sem.at[LINE_DY.index(dy)], dev(dy=dy))

    def row_to_sib(dy):
        return remote(rows.at[SLOTS.index((0, dy))], rows.at[SLOTS.index((1, dy))], S_ROW, row_sib_sem, dev(dc=1))

    def row_arrived(dy):
        wait_for(rows.at[SLOTS.index((0, dy))], row_sem.at[LINE_DY.index(dy)])

    def piece(s, half):
        return u.at[s, pl.ds(half * 128, 128), :]

    def along(half, d):
        return (d, 0) if half == 0 else (0, d)

    def push(s, half, axis, d):
        dx, dz = ORDER[s]
        t = STEP[((dx + d) % 4, dz) if axis == 0 else (dx, (dz + d) % 4)]
        remote(piece(s, half), piece(t, half), S_PLANE, own_sem.at[t, half], dev(dx=d) if axis == 0 else dev(dz=d)).start()

    def wait_half(s, half):
        wait_for(piece(s, half), own_sem.at[s, half])

    for half in (0, 1):
        for d in (1, 3):
            push(0, half, half, d)
    for half in (0, 1):
        push(0, half, half, 2)
    for dy in (1, 3, 2):
        row_copy(dy).start()
    for half in (1, 0):
        for d in (1, 3, 2):
            push(0, half, 1 - half, d)
    row_to_sib(0).start()
    for d in (1, 3, 2):
        for half in (0, 1):
            s = STEP[along(half, d)]
            wait_half(s, half)
            for f in (1, 3, 2):
                push(s, half, 1 - half, f)
        row_arrived(d)
        row_to_sib(d).start()
    wait_for(rows.at[pl.ds(0, 4)], row_sib_sem)
    for j, dc, dy in line:
        remote(enc.at[OWN], enc.at[j], S_ENC, enc_sem, dev(dy=dy, dc=dc)).start()

    scale = inverse_temp * LOG2E
    r_iota = lax.broadcasted_iota(jnp.int32, (BLK, BLK), 0)
    c_iota = lax.broadcasted_iota(jnp.int32, (BLK, BLK), 1)

    def arrive(i):
        @pl.when((i >= 1) & (i < 7))
        def _():
            half = lax.rem(i, 2)
            wait_for(u.at[i, pl.ds(pl.multiple_of(half * 128, 128), 128), :], own_sem.at[i, half])

        @pl.when(i >= 7)
        def _():
            wait_half(i, 0)
            wait_half(i, 1)

    def compute(blocks):
        for i in blocks:
            arrive(i)
        for i in blocks:
            block = u[i]
            u32[pl.ds(pl.multiple_of(i * BLK, BLK), BLK), :] = block.astype(F32)
            for j in range(LINE):
                dots = lax.dot_general(rows[j], block, (((1,), (1,)), ((), ())), preferred_element_type=F32)
                ex = jnp.exp2(dots * scale)
                if j == OWN:
                    ex = jnp.where(r_iota == c_iota + i * BLK, 0.0, ex)
                acc[j] += ex[:, :128] + ex[:, 128:]
                e[j, i] = ex.astype(BF16)

    def two(n, carry):
        compute((2 * n, 2 * n + 1))
        return carry

    def one(i, carry):
        compute((i,))
        return carry

    lax.fori_loop(0, TWOS, two, 0)
    lax.fori_loop(2 * TWOS, PLANE, one, 0)

    for j in range(LINE):
        rs_send[j] = transposed_sum(acc[j])
    for j, dc, dy in line:
        remote(rs_send.at[j], rs_recv.at[j], S_RS, rs_sem, dev(dy=-dy, dc=dc)).start()

    wait_for(enc.at[pl.ds(0, 7)], enc_sem)
    v = enc[...]
    index[...] = jnp.where((v >> 12) == y * 2 + core, v & (COLS - 1), COLS)
    to_smem = pltpu.make_async_copy(index, index_s, local_sem)
    to_smem.start()
    to_smem.wait()

    def fetch(j, carry):
        for t in range(BLK):
            pick[j, t : t + 1, :] = u32[pl.ds(index_s[j, 0, t], 1), :]
        return carry

    lax.fori_loop(0, FIRST, fetch, 0)

    wait_for(rs_recv.at[pl.ds(0, 7)], rs_sem)
    row_sums = rs_send[OWN]
    for j, dc, dy in line:
        row_sums += rs_recv[j]
    recip = 1.0 / row_sums
    r_cols[0] = recip
    r_rows[OWN] = recip
    for dx, dz in plane:
        remote(r_cols.at[0], r_cols.at[STEP[(dx, dz)]], S_RCOL, rcol_sem, dev(dx, dz)).start()
    for j, dc, dy in line:
        remote(r_cols.at[0], r_rows.at[j], S_RROW, rrow_sem, dev(dy=dy, dc=dc)).start()

    lax.fori_loop(FIRST, LINE, fetch, 0)
    for j in range(LINE):
        q = rows[j].astype(F32) * pick[j]
        pos_send[j] = transposed_sum(q[:, :128] + q[:, 128:]) * inverse_temp
    for j, dc, dy in line:
        remote(pos_send.at[j], pos_recv.at[j], S_POS, pos_sem, dev(dy=-dy, dc=dc)).start()

    wait_for(r_rows.at[pl.ds(0, 7)], rrow_sem)
    for j in range(LINE):
        r = r_rows[j]
        for h in (0, 1):
            part = jnp.broadcast_to(r[:, h * 128 : (h + 1) * 128], (128, 128))
            ri[j, h * 128 : (h + 1) * 128, :] = jnp.transpose(part)
    wait_for(r_cols.at[pl.ds(1, PLANE - 1)], rcol_sem)

    def weigh(j, carry):
        r_row = jnp.concatenate([ri[j], ri[j]], axis=1)
        total = jnp.zeros((BLK, PROJ), F32)
        for pos in range(PLANE):
            w = e[j, pos].astype(F32) * (r_row + r_cols[pos])
            total += jnp.dot(w.astype(BF16), u[pos], preferred_element_type=F32)
        g_own[...] = inverse_temp * (total - 2.0 * pick[j])
        for t, (dc, dy) in enumerate(SLOTS):

            @pl.when(j == t)
            def _():
                k = LINE_DY.index(dy)
                if dc:
                    s_send[k] = g_own[...].astype(BF16)
                    remote(s_send.at[k], s_recv.at[k], S_SIB, s_sem.at[k], dev(dc=1)).start()
                else:
                    wait_for(s_recv.at[k], s_sem.at[k])
                    if dy:
                        g_send[k] = (g_own[...] + s_recv[k].astype(F32)).astype(BF16)
                        remote(g_send.at[k], g_recv.at[k], S_G, g_sem, dev(dy=-dy)).start()

        return carry

    lax.fori_loop(0, LINE, weigh, 0)

    wait_for(pos_recv.at[pl.ds(0, 7)], pos_sem)
    positive = pos_send[OWN]
    for j, dc, dy in line:
        positive += pos_recv[j]
    loss_ref[...] = (jnp.log(row_sums) - positive).reshape(BLK)
    wait_for(g_recv.at[pl.ds(0, 3)], g_sem)
    grad_unit = g_own[...] + s_recv[3].astype(F32) + g_recv[0].astype(F32) + g_recv[1].astype(F32) + g_recv[2].astype(F32)
    inv_b = jnp.concatenate([inv[...], inv[...]], axis=1)
    unit = proj_ref[...] * inv_b
    along = jnp.sum(unit * grad_unit, axis=1, keepdims=True)
    grad_ref[...] = inv_b * (grad_unit - unit * along)

    for sem, ref, n in (
        (S_PLANE, u, 15), (S_ROW, rows, 7), (S_ENC, enc, 7), (S_RS, rs_send, 7), (S_RCOL, r_cols, 15), (S_RROW, r_rows, 7),
        (S_POS, pos_send, 7), (S_G, g_send, 3), (S_SIB, s_send, 4),
    ):
        wait_for(ref.at[pl.ds(0, n)], send_sem.at[sem])


def on_device(projections, partners):
    dma = pltpu.SemaphoreType.DMA
    vmem = pl.BlockSpec(memory_space=pltpu.VMEM)
    loss, grad = pl.pallas_call(
        kernel,
        out_shape=(jax.ShapeDtypeStruct((BLK,), F32), jax.ShapeDtypeStruct((BLK, PROJ), F32)),
        in_specs=[pl.BlockSpec(memory_space=pltpu.HBM)] * 2,
        out_specs=(vmem, vmem),
        scratch_shapes=[
            pltpu.VMEM((BLK, PROJ), F32),
            pltpu.VMEM((BLK,), jnp.int32),
            pltpu.VMEM((PLANE, BLK, PROJ), BF16),
            pltpu.VMEM((COLS + 8, PROJ), F32),
            pltpu.VMEM((LINE, BLK, PROJ), BF16),
            pltpu.VMEM((LINE, PLANE, BLK, BLK), BF16),
            pltpu.VMEM((LINE, BLK, 128), F32),
            pltpu.VMEM((BLK, 128), F32),
            pltpu.VMEM((LINE, 1, BLK), jnp.int32),
            pltpu.VMEM((LINE, 1, BLK), jnp.int32),
            pltpu.SMEM((LINE, 1, BLK), jnp.int32),
            pltpu.VMEM((LINE, BLK, PROJ), F32),
            pltpu.VMEM((LINE, 1, BLK), F32),
            pltpu.VMEM((LINE, 1, BLK), F32),
            pltpu.VMEM((PLANE, 1, BLK), F32),
            pltpu.VMEM((LINE, 1, BLK), F32),
            pltpu.VMEM((LINE, BLK, 128), F32),
            pltpu.VMEM((LINE, 1, BLK), F32),
            pltpu.VMEM((LINE, 1, BLK), F32),
            pltpu.VMEM((BLK, PROJ), F32),
            pltpu.VMEM((RING, BLK, PROJ), BF16),
            pltpu.VMEM((RING, BLK, PROJ), BF16),
            pltpu.VMEM((RING, BLK, PROJ), BF16),
            pltpu.VMEM((RING, BLK, PROJ), BF16),
            dma((16, 2)), dma((3,)), dma, dma, dma, dma, dma, dma, dma, dma((RING,)), dma((9,)), dma, dma((2,)),
        ],
        compiler_params=pltpu.CompilerParams(
            collective_id=0, has_side_effects=True, vmem_limit_bytes=54850 * 1024
        ),
        cost_estimate=pl.CostEstimate(flops=4 * LINE * BLK * COLS * PROJ, bytes_accessed=8 << 20, transcendentals=LINE * BLK * COLS),
    )(projections, partners)
    return loss, grad


def solution(mesh):
    return jax.shard_map(
        on_device,
        mesh=mesh,
        in_specs=(P(("loop", "group"), None), P(("loop", "group"))),
        out_specs=(P(("loop", "group")), P(("loop", "group"), None)),
        check_vma=False,
    )
```

```python
import jax
import jax.numpy as jnp
from jax import lax
from jax.experimental import pallas as pl
from jax.experimental.pallas import tpu as pltpu
from jax.sharding import PartitionSpec as P

MESH = pl.DeviceIdType.MESH
F32, BF16 = jnp.float32, jnp.bfloat16
epsilon = 1e-06
inverse_temp = 10.0
LOG2E = 1.4426950408889634

PROJ = 256
BLK = 256
RING = 4
PLANE = RING * RING
COLS = PLANE * BLK
LINE = 2 * RING

ORDER = [
    (0, 0), (1, 0), (0, 1), (3, 0), (0, 3), (2, 0), (0, 2), (1, 1),
    (3, 1), (1, 3), (3, 3), (1, 2), (3, 2), (2, 1), (2, 3), (2, 2),
]
STEP = {d: s for s, d in enumerate(ORDER)}
SLOTS = ((1, 2), (0, 2), (1, 1), (0, 1), (1, 3), (0, 3), (1, 0), (0, 0))
OWN = 7
TWOS = 7
FIRST = 3
S_PLANE, S_ROW, S_ENC, S_RS, S_RCOL, S_RROW, S_POS, S_G = range(8)


def transposed_sum(v):
    parts = [jnp.sum(jnp.transpose(v[i * 128 : (i + 1) * 128, :]), axis=0, keepdims=True) for i in range(2)]
    return jnp.concatenate(parts, axis=1)


def kernel(
    proj_hbm, part_hbm, loss_ref, grad_ref,
    proj_ref, part_ref, u, u32, rows, e, acc, inv, enc, index, index_s, pick,
    rs_send, rs_recv, r_cols, r_rows, ri, pos_send, pos_recv, g_own, g_send, g_recv,
    own_sem, row_sem, enc_sem, rs_sem, rcol_sem, rrow_sem, pos_sem, g_sem, send_sem, local_sem, in_sem,
):
    loop, group = lax.axis_index("loop"), lax.axis_index("group")
    core, z, x_lo = lax.rem(loop, 2), lax.rem(loop // 2, 4), loop // 8
    y, x_hi = group // 2, lax.rem(group, 2)
    x = x_hi * 2 + x_lo

    first = core == 0
    p, q = jnp.where(first, x, y), jnp.where(first, y, x)

    def dev(dp=0, dz=0, dq=0, dc=0):
        pp, qq, zz = lax.rem(p + dp + 4, 4), lax.rem(q + dq + 4, 4), lax.rem(z + dz + 4, 4)
        xx, yy = jnp.where(first, pp, qq), jnp.where(first, qq, pp)
        cc = 1 - core if dc else core
        return ((lax.rem(xx, 2) * 4 + zz) * 2 + cc, yy * 2 + xx // 2)

    def reader(dc, dq):
        return dev(dp=dq, dc=1) if dc else dev(dq=dq)

    def remote(src, dst, send, recv, to):
        return pltpu.make_async_remote_copy(
            src_ref=src, dst_ref=dst, send_sem=send_sem.at[send], recv_sem=recv, device_id=to, device_id_type=MESH
        )

    proj_in = pltpu.make_async_copy(proj_hbm, proj_ref, in_sem.at[0])
    part_in = pltpu.make_async_copy(part_hbm, part_ref, in_sem.at[1])
    proj_in.start()
    part_in.start()
    plane = [(dx, dz) for dz in (2, 1, 3, 0) for dx in (2, 1, 3, 0) if (dx, dz) != (0, 0)]
    line = [(j, dc, dq) for j, (dc, dq) in enumerate(SLOTS) if j != OWN]
    near = [dev(dp=k) for k in (1, 2, 3)] + [dev(dz=k) for k in (1, 2, 3)] + [dev(dq=k) for k in (1, 2, 3)]
    near += [dev(dq=k, dc=1) for k in (0, 1, 2, 3)]
    barrier = pltpu.get_barrier_semaphore()
    for to in near:
        pl.semaphore_signal(barrier, inc=1, device_id=to, device_id_type=MESH)

    proj_in.wait()
    proj = proj_ref[...]
    inv_norm = lax.rsqrt(jnp.sum(proj * proj, axis=1, keepdims=True) + epsilon)
    inv[...] = jnp.broadcast_to(inv_norm, inv.shape)
    low = (proj * inv_norm).astype(BF16)
    u[0] = low
    rows[OWN] = low
    part_in.wait()

    enc[OWN] = part_ref[...].reshape(1, BLK)
    u32[COLS : COLS + 8, :] = jnp.zeros((8, PROJ), F32)
    acc[...] = jnp.zeros_like(acc)

    pl.semaphore_wait(barrier, len(near))

    def wait_for(ref, sem):
        pltpu.make_async_copy(ref, ref, sem).wait()

    def piece(s, half):
        return u.at[s, pl.ds(half * 128, 128), :]

    def along(half, d):
        return (d, 0) if half == 0 else (0, d)

    def push(s, half, axis, d):
        dx, dz = ORDER[s]
        t = STEP[((dx + d) % 4, dz) if axis == 0 else (dx, (dz + d) % 4)]
        remote(piece(s, half), piece(t, half), S_PLANE, own_sem.at[t, half], dev(dp=d) if axis == 0 else dev(dz=d)).start()

    def wait_half(s, half):
        wait_for(piece(s, half), own_sem.at[s, half])

    for half in (0, 1):
        for d in (1, 3):
            push(0, half, half, d)
    for half in (0, 1):
        push(0, half, half, 2)
    for dq in (1, 3, 2, 0):
        for dc in (0, 1):
            if (dc, dq) != (0, 0):
                remote(u.at[0], rows.at[SLOTS.index((dc, dq))], S_ROW, row_sem, reader(dc, dq)).start()
    for half in (1, 0):
        for d in (1, 3, 2):
            push(0, half, 1 - half, d)
    for d in (1, 3, 2):
        for half in (0, 1):
            s = STEP[along(half, d)]
            wait_half(s, half)
            for f in (1, 3, 2):
                push(s, half, 1 - half, f)
    for j, dc, dq in line:
        remote(enc.at[OWN], enc.at[j], S_ENC, enc_sem, reader(dc, dq)).start()
    wait_for(rows.at[pl.ds(0, 7)], row_sem)

    scale = inverse_temp * LOG2E
    r_iota = lax.broadcasted_iota(jnp.int32, (BLK, BLK), 0)
    c_iota = lax.broadcasted_iota(jnp.int32, (BLK, BLK), 1)

    def arrive(i):
        @pl.when((i >= 1) & (i < 7))
        def _():
            half = lax.rem(i, 2)
            wait_for(u.at[i, pl.ds(pl.multiple_of(half * 128, 128), 128), :], own_sem.at[i, half])

        @pl.when(i >= 7)
        def _():
            wait_half(i, 0)
            wait_half(i, 1)

    def compute(blocks):
        for i in blocks:
            arrive(i)
        for i in blocks:
            block = u[i]
            u32[pl.ds(pl.multiple_of(i * BLK, BLK), BLK), :] = block.astype(F32)
            for j in range(LINE):
                dots = lax.dot_general(rows[j], block, (((1,), (1,)), ((), ())), preferred_element_type=F32)
                ex = jnp.exp2(dots * scale)
                if j == OWN:
                    ex = jnp.where(r_iota == c_iota + i * BLK, 0.0, ex)
                acc[j] += ex[:, :128] + ex[:, 128:]
                e[j, i] = ex.astype(BF16)

    def two(n, carry):
        compute((2 * n, 2 * n + 1))
        return carry

    def one(i, carry):
        compute((i,))
        return carry

    lax.fori_loop(0, TWOS, two, 0)
    lax.fori_loop(2 * TWOS, PLANE, one, 0)

    for j in range(LINE):
        rs_send[j] = transposed_sum(acc[j])
    for j, dc, dq in line:
        remote(rs_send.at[j], rs_recv.at[j], S_RS, rs_sem, dev(dq=-dq, dc=dc)).start()

    wait_for(enc.at[pl.ds(0, 7)], enc_sem)
    v = enc[...]
    off, v_group, v_loop = v & 255, (v >> 8) & 7, v >> 11
    v_x, v_y = ((v_group & 1) << 1) + (v_loop >> 3), v_group >> 1
    v_p, v_q = jnp.where(first, v_x, v_y), jnp.where(first, v_y, v_x)
    key = ((p - v_p) & 3) * 4 + ((z - (v_loop >> 1)) & 3)
    place = jnp.zeros_like(v)
    for d, t in STEP.items():
        place = jnp.where(key == d[0] * 4 + d[1], t, place)
    index[...] = jnp.where(((v_loop & 1) == core) & (v_q == q), place * BLK + off, COLS)
    to_smem = pltpu.make_async_copy(index, index_s, local_sem)
    to_smem.start()
    to_smem.wait()

    def fetch(j, carry):
        for t in range(BLK):
            pick[j, t : t + 1, :] = u32[pl.ds(index_s[j, 0, t], 1), :]
        return carry

    lax.fori_loop(0, FIRST, fetch, 0)

    wait_for(rs_recv.at[pl.ds(0, 7)], rs_sem)
    row_sums = rs_send[OWN]
    for j, dc, dq in line:
        row_sums += rs_recv[j]
    recip = 1.0 / row_sums
    r_cols[0] = recip
    r_rows[OWN] = recip
    for dx, dz in plane:
        remote(r_cols.at[0], r_cols.at[STEP[(dx, dz)]], S_RCOL, rcol_sem, dev(dx, dz)).start()
    for j, dc, dq in line:
        remote(r_cols.at[0], r_rows.at[j], S_RROW, rrow_sem, reader(dc, dq)).start()

    lax.fori_loop(FIRST, LINE, fetch, 0)
    for j in range(LINE):
        both = rows[j].astype(F32) * pick[j]
        pos_send[j] = transposed_sum(both[:, :128] + both[:, 128:]) * inverse_temp
    for j, dc, dq in line:
        remote(pos_send.at[j], pos_recv.at[j], S_POS, pos_sem, dev(dq=-dq, dc=dc)).start()

    wait_for(r_rows.at[pl.ds(0, 7)], rrow_sem)
    for j in range(LINE):
        r = r_rows[j]
        for h in (0, 1):
            part = jnp.broadcast_to(r[:, h * 128 : (h + 1) * 128], (128, 128))
            ri[j, h * 128 : (h + 1) * 128, :] = jnp.transpose(part)
    wait_for(r_cols.at[pl.ds(1, PLANE - 1)], rcol_sem)

    def weigh(j, carry):
        r_row = jnp.concatenate([ri[j], ri[j]], axis=1)
        total = jnp.zeros((BLK, PROJ), F32)
        for pos in range(PLANE):
            w = e[j, pos].astype(F32) * (r_row + r_cols[pos])
            total += jnp.dot(w.astype(BF16), u[pos], preferred_element_type=F32)
        g_own[...] = inverse_temp * (total - 2.0 * pick[j])
        g_send[j] = g_own[...].astype(BF16)
        for t, dc, dq in line:

            @pl.when(j == t)
            def _():
                remote(g_send.at[t], g_recv.at[t], S_G, g_sem, dev(dq=-dq, dc=dc)).start()

        return carry

    lax.fori_loop(0, LINE, weigh, 0)

    wait_for(pos_recv.at[pl.ds(0, 7)], pos_sem)
    positive = pos_send[OWN]
    for j, dc, dq in line:
        positive += pos_recv[j]
    loss_ref[...] = (jnp.log(row_sums) - positive).reshape(BLK)
    wait_for(g_recv.at[pl.ds(0, 7)], g_sem)
    grad_unit = g_own[...]
    for j, dc, dq in line:
        grad_unit += g_recv[j].astype(F32)
    inv_b = jnp.concatenate([inv[...], inv[...]], axis=1)
    unit = proj_ref[...] * inv_b
    along = jnp.sum(unit * grad_unit, axis=1, keepdims=True)
    grad_ref[...] = inv_b * (grad_unit - unit * along)

    for sem, ref, n in (
        (S_PLANE, u, 15), (S_ROW, rows, 7), (S_ENC, enc, 7), (S_RS, rs_send, 7), (S_RCOL, r_cols, 15), (S_RROW, r_rows, 7),
        (S_POS, pos_send, 7), (S_G, g_send, 7),
    ):
        wait_for(ref.at[pl.ds(0, n)], send_sem.at[sem])


def on_device(projections, partners):
    dma = pltpu.SemaphoreType.DMA
    vmem = pl.BlockSpec(memory_space=pltpu.VMEM)
    loss, grad = pl.pallas_call(
        kernel,
        out_shape=(jax.ShapeDtypeStruct((BLK,), F32), jax.ShapeDtypeStruct((BLK, PROJ), F32)),
        in_specs=[pl.BlockSpec(memory_space=pltpu.HBM)] * 2,
        out_specs=(vmem, vmem),
        scratch_shapes=[
            pltpu.VMEM((BLK, PROJ), F32),
            pltpu.VMEM((BLK,), jnp.int32),
            pltpu.VMEM((PLANE, BLK, PROJ), BF16),
            pltpu.VMEM((COLS + 8, PROJ), F32),
            pltpu.VMEM((LINE, BLK, PROJ), BF16),
            pltpu.VMEM((LINE, PLANE, BLK, BLK), BF16),
            pltpu.VMEM((LINE, BLK, 128), F32),
            pltpu.VMEM((BLK, 128), F32),
            pltpu.VMEM((LINE, 1, BLK), jnp.int32),
            pltpu.VMEM((LINE, 1, BLK), jnp.int32),
            pltpu.SMEM((LINE, 1, BLK), jnp.int32),
            pltpu.VMEM((LINE, BLK, PROJ), F32),
            pltpu.VMEM((LINE, 1, BLK), F32),
            pltpu.VMEM((LINE, 1, BLK), F32),
            pltpu.VMEM((PLANE, 1, BLK), F32),
            pltpu.VMEM((LINE, 1, BLK), F32),
            pltpu.VMEM((LINE, BLK, 128), F32),
            pltpu.VMEM((LINE, 1, BLK), F32),
            pltpu.VMEM((LINE, 1, BLK), F32),
            pltpu.VMEM((BLK, PROJ), F32),
            pltpu.VMEM((LINE, BLK, PROJ), BF16),
            pltpu.VMEM((LINE, BLK, PROJ), BF16),
            dma((16, 2)), dma, dma, dma, dma, dma, dma, dma, dma((8,)), dma, dma((2,)),
        ],
        compiler_params=pltpu.CompilerParams(
            collective_id=0, has_side_effects=True, vmem_limit_bytes=54850 * 1024
        ),
        cost_estimate=pl.CostEstimate(flops=4 * LINE * BLK * COLS * PROJ, bytes_accessed=8 << 20, transcendentals=LINE * BLK * COLS),
    )(projections, partners)
    return loss, grad


def solution(mesh):
    return jax.shard_map(
        on_device,
        mesh=mesh,
        in_specs=(P(("loop", "group"), None), P(("loop", "group"))),
        out_specs=(P(("loop", "group")), P(("loop", "group"), None)),
        check_vma=False,
    )
```

```python
import jax
import jax.numpy as jnp
from jax import lax
from jax.experimental import pallas as pl
from jax.experimental.pallas import tpu as pltpu
from jax.sharding import PartitionSpec as P

MESH = pl.DeviceIdType.MESH
F32, BF16 = jnp.float32, jnp.bfloat16
epsilon = 1e-06
inverse_temp = 10.0
LOG2E = 1.4426950408889634

PROJ = 256
BLK = 256
RING = 4
PLANE = RING * RING
COLS = PLANE * BLK
LINE = 2 * RING

ORDER = [
    (0, 0), (1, 0), (0, 1), (3, 0), (0, 3), (2, 0), (0, 2), (1, 1),
    (3, 1), (1, 3), (3, 3), (1, 2), (3, 2), (2, 1), (2, 3), (2, 2),
]
STEP = {d: s for s, d in enumerate(ORDER)}
SLOTS = ((1, 2), (0, 2), (1, 1), (0, 1), (1, 3), (0, 3), (1, 0), (0, 0))
OWN = 7
CUT = 112
TWOS = 7
FIRST = 3
S_PLANE, S_ROW, S_ENC, S_RS, S_RCOL, S_RROW, S_POS, S_G = range(8)


def transposed_sum(v):
    parts = [jnp.sum(jnp.transpose(v[i * 128 : (i + 1) * 128, :]), axis=0, keepdims=True) for i in range(2)]
    return jnp.concatenate(parts, axis=1)


def kernel(
    proj_hbm, part_hbm, loss_ref, grad_ref,
    proj_ref, part_ref, u, u32, rows, e, acc, inv, enc, index, index_s, pick,
    rs_send, rs_recv, r_cols, r_rows, ri, pos_send, pos_recv, g_own, g_send, g_recv,
    own_sem, row_sem, enc_sem, rs_sem, rcol_sem, rrow_sem, pos_sem, g_sem, send_sem, local_sem, in_sem,
):
    loop, group = lax.axis_index("loop"), lax.axis_index("group")
    core, z, x_lo = lax.rem(loop, 2), lax.rem(loop // 2, 4), loop // 8
    y, x_hi = group // 2, lax.rem(group, 2)
    x = x_hi * 2 + x_lo

    first = core == 0
    p, q = jnp.where(first, x, y), jnp.where(first, y, x)

    def dev(dp=0, dz=0, dq=0, dc=0):
        pp, qq, zz = lax.rem(p + dp + 4, 4), lax.rem(q + dq + 4, 4), lax.rem(z + dz + 4, 4)
        xx, yy = jnp.where(first, pp, qq), jnp.where(first, qq, pp)
        cc = 1 - core if dc else core
        return ((lax.rem(xx, 2) * 4 + zz) * 2 + cc, yy * 2 + xx // 2)

    def reader(dc, dq):
        return dev(dp=dq, dc=1) if dc else dev(dq=dq)

    def remote(src, dst, send, recv, to):
        return pltpu.make_async_remote_copy(
            src_ref=src, dst_ref=dst, send_sem=send_sem.at[send], recv_sem=recv, device_id=to, device_id_type=MESH
        )

    proj_in = pltpu.make_async_copy(proj_hbm, proj_ref, in_sem.at[0])
    part_in = pltpu.make_async_copy(part_hbm, part_ref, in_sem.at[1])
    proj_in.start()
    part_in.start()
    plane = [(dx, dz) for dz in (2, 1, 3, 0) for dx in (2, 1, 3, 0) if (dx, dz) != (0, 0)]
    line = [(j, dc, dq) for j, (dc, dq) in enumerate(SLOTS) if j != OWN]
    near = [dev(dp=k) for k in (1, 2, 3)] + [dev(dz=k) for k in (1, 2, 3)] + [dev(dq=k) for k in (1, 2, 3)]
    near += [dev(dq=k, dc=1) for k in (0, 1, 2, 3)]
    barrier = pltpu.get_barrier_semaphore()
    for to in near:
        pl.semaphore_signal(barrier, inc=1, device_id=to, device_id_type=MESH)

    proj_in.wait()
    proj = proj_ref[...]
    inv_norm = lax.rsqrt(jnp.sum(proj * proj, axis=1, keepdims=True) + epsilon)
    inv[...] = jnp.broadcast_to(inv_norm, inv.shape)
    low = (proj * inv_norm).astype(BF16)
    u[0] = low
    rows[OWN] = low
    part_in.wait()

    enc[OWN] = part_ref[...].reshape(1, BLK)
    u32[COLS : COLS + 8, :] = jnp.zeros((8, PROJ), F32)
    acc[...] = jnp.zeros_like(acc)

    pl.semaphore_wait(barrier, len(near))

    def wait_for(ref, sem):
        pltpu.make_async_copy(ref, ref, sem).wait()

    def piece(s, half):
        return u.at[s, pl.ds(half * CUT, BLK - CUT if half else CUT), :]

    def along(half, d):
        return (d, 0) if half == 0 else (0, d)

    def push(s, half, axis, d):
        dx, dz = ORDER[s]
        t = STEP[((dx + d) % 4, dz) if axis == 0 else (dx, (dz + d) % 4)]
        remote(piece(s, half), piece(t, half), S_PLANE, own_sem.at[t, half], dev(dp=d) if axis == 0 else dev(dz=d)).start()

    def wait_half(s, half):
        wait_for(piece(s, half), own_sem.at[s, half])

    for half in (0, 1):
        for d in (1, 3):
            push(0, half, half, d)
    for half in (0, 1):
        push(0, half, half, 2)
    for dq in (1, 3, 2, 0):
        for dc in (0, 1):
            if (dc, dq) != (0, 0):
                remote(u.at[0], rows.at[SLOTS.index((dc, dq))], S_ROW, row_sem, reader(dc, dq)).start()
    for half in (1, 0):
        for d in (1, 3, 2):
            push(0, half, 1 - half, d)
    for d in (1, 3, 2):
        for half in (0, 1):
            s = STEP[along(half, d)]
            wait_half(s, half)
            for f in (1, 3, 2):
                push(s, half, 1 - half, f)
    for j, dc, dq in line:
        remote(enc.at[OWN], enc.at[j], S_ENC, enc_sem, reader(dc, dq)).start()
    wait_for(rows.at[pl.ds(0, 7)], row_sem)

    scale = inverse_temp * LOG2E
    r_iota = lax.broadcasted_iota(jnp.int32, (BLK, BLK), 0)
    c_iota = lax.broadcasted_iota(jnp.int32, (BLK, BLK), 1)

    def arrive(i):
        @pl.when((i >= 7) | ((i > 0) & (lax.rem(i, 2) == 0)))
        def _():
            wait_half(i, 0)

        @pl.when((i >= 7) | (lax.rem(i, 2) == 1))
        def _():
            wait_half(i, 1)

    def compute(blocks):
        for i in blocks:
            arrive(i)
        for i in blocks:
            block = u[i]
            u32[pl.ds(pl.multiple_of(i * BLK, BLK), BLK), :] = block.astype(F32)
            for j in range(LINE):
                dots = lax.dot_general(rows[j], block, (((1,), (1,)), ((), ())), preferred_element_type=F32)
                ex = jnp.exp2(dots * scale)
                if j == OWN:
                    ex = jnp.where(r_iota == c_iota + i * BLK, 0.0, ex)
                acc[j] += ex[:, :128] + ex[:, 128:]
                e[j, i] = ex.astype(BF16)

    def two(n, carry):
        compute((2 * n, 2 * n + 1))
        return carry

    def one(i, carry):
        compute((i,))
        return carry

    lax.fori_loop(0, TWOS, two, 0)
    lax.fori_loop(2 * TWOS, PLANE, one, 0)

    for j, (dc, dq) in enumerate(SLOTS):
        rs_send[j] = transposed_sum(acc[j])
        if j != OWN:
            remote(rs_send.at[j], rs_recv.at[j], S_RS, rs_sem, dev(dq=-dq, dc=dc)).start()

    wait_for(enc.at[pl.ds(0, 7)], enc_sem)
    v = enc[...]
    off, v_group, v_loop = v & 255, (v >> 8) & 7, v >> 11
    v_x, v_y = ((v_group & 1) << 1) + (v_loop >> 3), v_group >> 1
    v_p, v_q = jnp.where(first, v_x, v_y), jnp.where(first, v_y, v_x)
    key = ((p - v_p) & 3) * 4 + ((z - (v_loop >> 1)) & 3)
    place = jnp.zeros_like(v)
    for d, t in STEP.items():
        place = jnp.where(key == d[0] * 4 + d[1], t, place)
    index[...] = jnp.where(((v_loop & 1) == core) & (v_q == q), place * BLK + off, COLS)
    to_smem = pltpu.make_async_copy(index, index_s, local_sem)
    to_smem.start()
    to_smem.wait()

    def fetch(j, carry):
        for t in range(BLK):
            pick[j, t : t + 1, :] = u32[pl.ds(index_s[j, 0, t], 1), :]
        return carry

    lax.fori_loop(0, FIRST, fetch, 0)

    wait_for(rs_recv.at[pl.ds(0, 7)], rs_sem)
    row_sums = rs_send[OWN]
    for j, dc, dq in line:
        row_sums += rs_recv[j]
    recip = 1.0 / row_sums
    r_cols[0] = recip
    r_rows[OWN] = recip
    for dx, dz in plane:
        remote(r_cols.at[0], r_cols.at[STEP[(dx, dz)]], S_RCOL, rcol_sem, dev(dx, dz)).start()
    for j, dc, dq in line:
        remote(r_cols.at[0], r_rows.at[j], S_RROW, rrow_sem, reader(dc, dq)).start()

    lax.fori_loop(FIRST, LINE, fetch, 0)
    for j in range(LINE):
        both = rows[j].astype(F32) * pick[j]
        pos_send[j] = transposed_sum(both[:, :128] + both[:, 128:]) * inverse_temp
    for j, dc, dq in line:
        remote(pos_send.at[j], pos_recv.at[j], S_POS, pos_sem, dev(dq=-dq, dc=dc)).start()

    wait_for(r_rows.at[pl.ds(0, 7)], rrow_sem)
    for j in range(LINE):
        r = r_rows[j]
        for h in (0, 1):
            part = jnp.broadcast_to(r[:, h * 128 : (h + 1) * 128], (128, 128))
            ri[j, h * 128 : (h + 1) * 128, :] = jnp.transpose(part)
    wait_for(r_cols.at[pl.ds(1, PLANE - 1)], rcol_sem)

    def weigh(j, carry):
        r_row = jnp.concatenate([ri[j], ri[j]], axis=1)
        total = jnp.zeros((BLK, PROJ), F32)
        for pos in range(PLANE):
            w = e[j, pos].astype(F32) * (r_row + r_cols[pos])
            total += jnp.dot(w.astype(BF16), u[pos], preferred_element_type=F32)
        g_own[...] = inverse_temp * (total - 2.0 * pick[j])
        g_send[j] = g_own[...].astype(BF16)
        for t, dc, dq in line:

            @pl.when(j == t)
            def _():
                remote(g_send.at[t], g_recv.at[t], S_G, g_sem, dev(dq=-dq, dc=dc)).start()

        return carry

    lax.fori_loop(0, LINE, weigh, 0)

    wait_for(pos_recv.at[pl.ds(0, 7)], pos_sem)
    positive = pos_send[OWN]
    for j, dc, dq in line:
        positive += pos_recv[j]
    loss_ref[...] = (jnp.log(row_sums) - positive).reshape(BLK)
    wait_for(g_recv.at[pl.ds(0, 7)], g_sem)
    grad_unit = g_own[...]
    for j, dc, dq in line:
        grad_unit += g_recv[j].astype(F32)
    inv_b = jnp.concatenate([inv[...], inv[...]], axis=1)
    unit = proj_ref[...] * inv_b
    along = jnp.sum(unit * grad_unit, axis=1, keepdims=True)
    grad_ref[...] = inv_b * (grad_unit - unit * along)

    for sem, ref, n in (
        (S_PLANE, u, 15), (S_ROW, rows, 7), (S_ENC, enc, 7), (S_RS, rs_send, 7), (S_RCOL, r_cols, 15), (S_RROW, r_rows, 7),
        (S_POS, pos_send, 7), (S_G, g_send, 7),
    ):
        wait_for(ref.at[pl.ds(0, n)], send_sem.at[sem])


def on_device(projections, partners):
    dma = pltpu.SemaphoreType.DMA
    vmem = pl.BlockSpec(memory_space=pltpu.VMEM)
    loss, grad = pl.pallas_call(
        kernel,
        out_shape=(jax.ShapeDtypeStruct((BLK,), F32), jax.ShapeDtypeStruct((BLK, PROJ), F32)),
        in_specs=[pl.BlockSpec(memory_space=pltpu.HBM)] * 2,
        out_specs=(vmem, vmem),
        scratch_shapes=[
            pltpu.VMEM((BLK, PROJ), F32),
            pltpu.VMEM((BLK,), jnp.int32),
            pltpu.VMEM((PLANE, BLK, PROJ), BF16),
            pltpu.VMEM((COLS + 8, PROJ), F32),
            pltpu.VMEM((LINE, BLK, PROJ), BF16),
            pltpu.VMEM((LINE, PLANE, BLK, BLK), BF16),
            pltpu.VMEM((LINE, BLK, 128), F32),
            pltpu.VMEM((BLK, 128), F32),
            pltpu.VMEM((LINE, 1, BLK), jnp.int32),
            pltpu.VMEM((LINE, 1, BLK), jnp.int32),
            pltpu.SMEM((LINE, 1, BLK), jnp.int32),
            pltpu.VMEM((LINE, BLK, PROJ), F32),
            pltpu.VMEM((LINE, 1, BLK), F32),
            pltpu.VMEM((LINE, 1, BLK), F32),
            pltpu.VMEM((PLANE, 1, BLK), F32),
            pltpu.VMEM((LINE, 1, BLK), F32),
            pltpu.VMEM((LINE, BLK, 128), F32),
            pltpu.VMEM((LINE, 1, BLK), F32),
            pltpu.VMEM((LINE, 1, BLK), F32),
            pltpu.VMEM((BLK, PROJ), F32),
            pltpu.VMEM((LINE, BLK, PROJ), BF16),
            pltpu.VMEM((LINE, BLK, PROJ), BF16),
            dma((16, 2)), dma, dma, dma, dma, dma, dma, dma, dma((8,)), dma, dma((2,)),
        ],
        compiler_params=pltpu.CompilerParams(
            collective_id=0, has_side_effects=True, vmem_limit_bytes=54850 * 1024
        ),
        cost_estimate=pl.CostEstimate(flops=4 * LINE * BLK * COLS * PROJ, bytes_accessed=8 << 20, transcendentals=LINE * BLK * COLS),
    )(projections, partners)
    return loss, grad


def solution(mesh):
    return jax.shard_map(
        on_device,
        mesh=mesh,
        in_specs=(P(("loop", "group"), None), P(("loop", "group"))),
        out_specs=(P(("loop", "group")), P(("loop", "group"), None)),
        check_vma=False,
    )
```

```python
import jax
import jax.numpy as jnp
from jax import lax
from jax.experimental import pallas as pl
from jax.experimental.pallas import tpu as pltpu
from jax.sharding import PartitionSpec as P

MESH = pl.DeviceIdType.MESH
F32, BF16 = jnp.float32, jnp.bfloat16
epsilon = 1e-06
inverse_temp = 10.0
LOG2E = 1.4426950408889634

PROJ = 256
BLK = 256
RING = 4
PLANE = RING * RING
COLS = PLANE * BLK
LINE = 2 * RING

ORDER = [
    (0, 0), (1, 0), (0, 1), (3, 0), (0, 3), (2, 0), (0, 2), (1, 1),
    (3, 1), (1, 3), (3, 3), (1, 2), (3, 2), (2, 1), (2, 3), (2, 2),
]
STEP = {d: s for s, d in enumerate(ORDER)}
SLOTS = ((1, 2), (0, 2), (1, 1), (0, 1), (1, 3), (0, 3), (1, 0), (0, 0))
OWN = 7
CUT = 112
TWOS = 7
FIRST = 3
S_PLANE, S_ROW, S_ENC, S_RS, S_RCOL, S_RROW, S_POS, S_G = range(8)


def transposed_sum(v):
    parts = [jnp.sum(jnp.transpose(v[i * 128 : (i + 1) * 128, :]), axis=0, keepdims=True) for i in range(2)]
    return jnp.concatenate(parts, axis=1)


def kernel(
    proj_hbm, part_hbm, loss_ref, grad_ref,
    proj_ref, part_ref, u, u32, rows, e, acc, inv, enc, index, index_s, pick,
    rs_send, rs_recv, r_cols, r_rows, ri, pos_send, pos_recv, g_own, g_send, g_recv,
    own_sem, row_sem, enc_sem, rs_sem, rcol_sem, rrow_sem, pos_sem, g_sem, send_sem, local_sem, in_sem,
):
    loop, group = lax.axis_index("loop"), lax.axis_index("group")
    core, z, x_lo = lax.rem(loop, 2), lax.rem(loop // 2, 4), loop // 8
    y, x_hi = group // 2, lax.rem(group, 2)
    x = x_hi * 2 + x_lo

    first = core == 0
    p, q = jnp.where(first, x, y), jnp.where(first, y, x)

    def dev(dp=0, dz=0, dq=0, dc=0):
        pp, qq, zz = lax.rem(p + dp + 4, 4), lax.rem(q + dq + 4, 4), lax.rem(z + dz + 4, 4)
        xx, yy = jnp.where(first, pp, qq), jnp.where(first, qq, pp)
        cc = 1 - core if dc else core
        return ((lax.rem(xx, 2) * 4 + zz) * 2 + cc, yy * 2 + xx // 2)

    def reader(dc, dq):
        return dev(dp=dq, dc=1) if dc else dev(dq=dq)

    def remote(src, dst, send, recv, to):
        return pltpu.make_async_remote_copy(
            src_ref=src, dst_ref=dst, send_sem=send_sem.at[send], recv_sem=recv, device_id=to, device_id_type=MESH
        )

    proj_in = pltpu.make_async_copy(proj_hbm, proj_ref, in_sem.at[0])
    part_in = pltpu.make_async_copy(part_hbm, part_ref, in_sem.at[1])
    proj_in.start()
    part_in.start()
    plane = [(dx, dz) for dz in (2, 1, 3, 0) for dx in (2, 1, 3, 0) if (dx, dz) != (0, 0)]
    line = [(j, dc, dq) for j, (dc, dq) in enumerate(SLOTS) if j != OWN]
    near = [dev(dp=k) for k in (1, 2, 3)] + [dev(dz=k) for k in (1, 2, 3)] + [dev(dq=k) for k in (1, 2, 3)]
    near += [dev(dc=1)]
    barrier = pltpu.get_barrier_semaphore()
    for to in near:
        pl.semaphore_signal(barrier, inc=1, device_id=to, device_id_type=MESH)

    proj_in.wait()
    proj = proj_ref[...]
    inv_norm = lax.rsqrt(jnp.sum(proj * proj, axis=1, keepdims=True) + epsilon)
    inv[...] = jnp.broadcast_to(inv_norm, inv.shape)
    low = (proj * inv_norm).astype(BF16)
    u[0] = low
    rows[OWN] = low
    part_in.wait()

    enc[OWN] = part_ref[...].reshape(1, BLK)
    u32[COLS : COLS + 8, :] = jnp.zeros((8, PROJ), F32)
    acc[...] = jnp.zeros_like(acc)

    pl.semaphore_wait(barrier, len(near))

    def wait_for(ref, sem):
        pltpu.make_async_copy(ref, ref, sem).wait()

    def piece(s, half):
        return u.at[s, pl.ds(half * CUT, BLK - CUT if half else CUT), :]

    def along(half, d):
        return (d, 0) if half == 0 else (0, d)

    def push(s, half, axis, d):
        dx, dz = ORDER[s]
        t = STEP[((dx + d) % 4, dz) if axis == 0 else (dx, (dz + d) % 4)]
        remote(piece(s, half), piece(t, half), S_PLANE, own_sem.at[t, half], dev(dp=d) if axis == 0 else dev(dz=d)).start()

    def wait_half(s, half):
        wait_for(piece(s, half), own_sem.at[s, half])

    for half in (0, 1):
        for d in (1, 3):
            push(0, half, half, d)
    for half in (0, 1):
        push(0, half, half, 2)
    for dc, dq in ((0, 1), (0, 3), (0, 2), (1, 0)):
        remote(u.at[0], rows.at[SLOTS.index((dc, dq))], S_ROW, row_sem, reader(dc, dq)).start()
    for half in (1, 0):
        for d in (1, 3, 2):
            push(0, half, 1 - half, d)
    for d in (1, 3, 2):
        for half in (0, 1):
            s = STEP[along(half, d)]
            wait_half(s, half)
            for f in (1, 3, 2):
                push(s, half, 1 - half, f)
    for d in (1, 3, 2):
        s = STEP[(d, 0)]
        wait_half(s, 1)
        remote(u.at[s], rows.at[SLOTS.index((1, d))], S_ROW, row_sem, dev(dc=1)).start()
    for j, dc, dq in line:
        remote(enc.at[OWN], enc.at[j], S_ENC, enc_sem, reader(dc, dq)).start()
    wait_for(rows.at[pl.ds(0, 7)], row_sem)

    scale = inverse_temp * LOG2E
    r_iota = lax.broadcasted_iota(jnp.int32, (BLK, BLK), 0)
    c_iota = lax.broadcasted_iota(jnp.int32, (BLK, BLK), 1)

    def arrive(i):
        @pl.when((i >= 7) | ((i > 0) & (lax.rem(i, 2) == 0)))
        def _():
            wait_half(i, 0)

        @pl.when(i >= 7)
        def _():
            wait_half(i, 1)

    def compute(blocks):
        for i in blocks:
            arrive(i)
        for i in blocks:
            block = u[i]
            u32[pl.ds(pl.multiple_of(i * BLK, BLK), BLK), :] = block.astype(F32)
            for j in range(LINE):
                dots = lax.dot_general(rows[j], block, (((1,), (1,)), ((), ())), preferred_element_type=F32)
                ex = jnp.exp2(dots * scale)
                if j == OWN:
                    ex = jnp.where(r_iota == c_iota + i * BLK, 0.0, ex)
                acc[j] += ex[:, :128] + ex[:, 128:]
                e[j, i] = ex.astype(BF16)

    def two(n, carry):
        compute((2 * n, 2 * n + 1))
        return carry

    def one(i, carry):
        compute((i,))
        return carry

    lax.fori_loop(0, TWOS, two, 0)
    lax.fori_loop(2 * TWOS, PLANE, one, 0)

    for j, (dc, dq) in enumerate(SLOTS):
        rs_send[j] = transposed_sum(acc[j])
        if j != OWN:
            remote(rs_send.at[j], rs_recv.at[j], S_RS, rs_sem, dev(dq=-dq, dc=dc)).start()

    wait_for(enc.at[pl.ds(0, 7)], enc_sem)
    v = enc[...]
    off, v_group, v_loop = v & 255, (v >> 8) & 7, v >> 11
    v_x, v_y = ((v_group & 1) << 1) + (v_loop >> 3), v_group >> 1
    v_p, v_q = jnp.where(first, v_x, v_y), jnp.where(first, v_y, v_x)
    key = ((p - v_p) & 3) * 4 + ((z - (v_loop >> 1)) & 3)
    place = jnp.zeros_like(v)
    for d, t in STEP.items():
        place = jnp.where(key == d[0] * 4 + d[1], t, place)
    index[...] = jnp.where(((v_loop & 1) == core) & (v_q == q), place * BLK + off, COLS)
    to_smem = pltpu.make_async_copy(index, index_s, local_sem)
    to_smem.start()
    to_smem.wait()

    def fetch(j, carry):
        for t in range(BLK):
            pick[j, t : t + 1, :] = u32[pl.ds(index_s[j, 0, t], 1), :]
        return carry

    lax.fori_loop(0, FIRST, fetch, 0)

    wait_for(rs_recv.at[pl.ds(0, 7)], rs_sem)
    row_sums = rs_send[OWN]
    for j, dc, dq in line:
        row_sums += rs_recv[j]
    recip = 1.0 / row_sums
    r_cols[0] = recip
    r_rows[OWN] = recip
    for dx, dz in plane:
        remote(r_cols.at[0], r_cols.at[STEP[(dx, dz)]], S_RCOL, rcol_sem, dev(dx, dz)).start()
    for j, dc, dq in line:
        remote(r_cols.at[0], r_rows.at[j], S_RROW, rrow_sem, reader(dc, dq)).start()

    lax.fori_loop(FIRST, LINE, fetch, 0)
    for j in range(LINE):
        both = rows[j].astype(F32) * pick[j]
        pos_send[j] = transposed_sum(both[:, :128] + both[:, 128:]) * inverse_temp
    for j, dc, dq in line:
        remote(pos_send.at[j], pos_recv.at[j], S_POS, pos_sem, dev(dq=-dq, dc=dc)).start()

    wait_for(r_rows.at[pl.ds(0, 7)], rrow_sem)
    for j in range(LINE):
        r = r_rows[j]
        for h in (0, 1):
            part = jnp.broadcast_to(r[:, h * 128 : (h + 1) * 128], (128, 128))
            ri[j, h * 128 : (h + 1) * 128, :] = jnp.transpose(part)
    wait_for(r_cols.at[pl.ds(1, PLANE - 1)], rcol_sem)

    def weigh(j, carry):
        r_row = jnp.concatenate([ri[j], ri[j]], axis=1)
        total = jnp.zeros((BLK, PROJ), F32)
        for pos in range(PLANE):
            w = e[j, pos].astype(F32) * (r_row + r_cols[pos])
            total += jnp.dot(w.astype(BF16), u[pos], preferred_element_type=F32)
        g_own[...] = inverse_temp * (total - 2.0 * pick[j])
        g_send[j] = g_own[...].astype(BF16)
        for t, dc, dq in line:

            @pl.when(j == t)
            def _():
                remote(g_send.at[t], g_recv.at[t], S_G, g_sem.at[t], dev(dq=-dq, dc=dc)).start()

        return carry

    lax.fori_loop(0, LINE, weigh, 0)

    wait_for(pos_recv.at[pl.ds(0, 7)], pos_sem)
    positive = pos_send[OWN]
    for j, dc, dq in line:
        positive += pos_recv[j]
    loss_ref[...] = (jnp.log(row_sums) - positive).reshape(BLK)
    for j in (6, 0, 1, 2, 3, 4, 5):
        wait_for(g_recv.at[j], g_sem.at[j])
        g_own[...] += g_recv[j].astype(F32)
    grad_unit = g_own[...]
    inv_b = jnp.concatenate([inv[...], inv[...]], axis=1)
    unit = proj_ref[...] * inv_b
    along = jnp.sum(unit * grad_unit, axis=1, keepdims=True)
    grad_ref[...] = inv_b * (grad_unit - unit * along)

    for sem, ref, n in (
        (S_PLANE, u, 15), (S_ROW, rows, 7), (S_ENC, enc, 7), (S_RS, rs_send, 7), (S_RCOL, r_cols, 15), (S_RROW, r_rows, 7),
        (S_POS, pos_send, 7), (S_G, g_send, 7),
    ):
        wait_for(ref.at[pl.ds(0, n)], send_sem.at[sem])


def on_device(projections, partners):
    dma = pltpu.SemaphoreType.DMA
    vmem = pl.BlockSpec(memory_space=pltpu.VMEM)
    loss, grad = pl.pallas_call(
        kernel,
        out_shape=(jax.ShapeDtypeStruct((BLK,), F32), jax.ShapeDtypeStruct((BLK, PROJ), F32)),
        in_specs=[pl.BlockSpec(memory_space=pltpu.HBM)] * 2,
        out_specs=(vmem, vmem),
        scratch_shapes=[
            pltpu.VMEM((BLK, PROJ), F32),
            pltpu.VMEM((BLK,), jnp.int32),
            pltpu.VMEM((PLANE, BLK, PROJ), BF16),
            pltpu.VMEM((COLS + 8, PROJ), F32),
            pltpu.VMEM((LINE, BLK, PROJ), BF16),
            pltpu.VMEM((LINE, PLANE, BLK, BLK), BF16),
            pltpu.VMEM((LINE, BLK, 128), F32),
            pltpu.VMEM((BLK, 128), F32),
            pltpu.VMEM((LINE, 1, BLK), jnp.int32),
            pltpu.VMEM((LINE, 1, BLK), jnp.int32),
            pltpu.SMEM((LINE, 1, BLK), jnp.int32),
            pltpu.VMEM((LINE, BLK, PROJ), F32),
            pltpu.VMEM((LINE, 1, BLK), F32),
            pltpu.VMEM((LINE, 1, BLK), F32),
            pltpu.VMEM((PLANE, 1, BLK), F32),
            pltpu.VMEM((LINE, 1, BLK), F32),
            pltpu.VMEM((LINE, BLK, 128), F32),
            pltpu.VMEM((LINE, 1, BLK), F32),
            pltpu.VMEM((LINE, 1, BLK), F32),
            pltpu.VMEM((BLK, PROJ), F32),
            pltpu.VMEM((LINE, BLK, PROJ), BF16),
            pltpu.VMEM((LINE, BLK, PROJ), BF16),
            dma((16, 2)), dma, dma, dma, dma, dma, dma, dma((7,)), dma((8,)), dma, dma((2,)),
        ],
        compiler_params=pltpu.CompilerParams(
            collective_id=0, has_side_effects=True, vmem_limit_bytes=54850 * 1024
        ),
        cost_estimate=pl.CostEstimate(flops=4 * LINE * BLK * COLS * PROJ, bytes_accessed=8 << 20, transcendentals=LINE * BLK * COLS),
    )(projections, partners)
    return loss, grad


def solution(mesh):
    return jax.shard_map(
        on_device,
        mesh=mesh,
        in_specs=(P(("loop", "group"), None), P(("loop", "group"))),
        out_specs=(P(("loop", "group")), P(("loop", "group"), None)),
        check_vma=False,
    )
```

```python
import jax
import jax.numpy as jnp
from jax import lax
from jax.experimental import pallas as pl
from jax.experimental.pallas import tpu as pltpu
from jax.sharding import PartitionSpec as P

MESH = pl.DeviceIdType.MESH
F32, BF16 = jnp.float32, jnp.bfloat16
epsilon = 1e-06
inverse_temp = 10.0
LOG2E = 1.4426950408889634

PROJ = 256
BLK = 256
RING = 4
PLANE = RING * RING
COLS = PLANE * BLK
LINE = 2 * RING

ORDER = [
    (0, 0), (1, 0), (0, 1), (3, 0), (0, 3), (2, 0), (0, 2), (1, 1),
    (3, 1), (1, 3), (3, 3), (1, 2), (3, 2), (2, 1), (2, 3), (2, 2),
]
STEP = {d: s for s, d in enumerate(ORDER)}
SLOTS = ((1, 2), (0, 2), (1, 1), (0, 1), (1, 3), (0, 3), (1, 0), (0, 0))
OWN = 7
CUT = 112
FIRST = 3
S_PLANE, S_ROW, S_ENC, S_RS, S_RCOL, S_RROW, S_POS, S_G = range(8)


def transposed_sum(v):
    parts = [jnp.sum(jnp.transpose(v[i * 128 : (i + 1) * 128, :]), axis=0, keepdims=True) for i in range(2)]
    return jnp.concatenate(parts, axis=1)


def kernel(
    proj_hbm, part_hbm, loss_ref, grad_ref,
    proj_ref, part_ref, u, u32, rows, e, acc, inv, enc, index, index_s, pick,
    rs_send, rs_recv, r_cols, r_rows, ri, pos_send, pos_recv, g_own, g_send, g_recv,
    own_sem, row_sem, enc_sem, rs_sem, rcol_sem, rrow_sem, pos_sem, g_sem, send_sem, local_sem, in_sem,
):
    loop, group = lax.axis_index("loop"), lax.axis_index("group")
    core, z, x_lo = lax.rem(loop, 2), lax.rem(loop // 2, 4), loop // 8
    y, x_hi = group // 2, lax.rem(group, 2)
    x = x_hi * 2 + x_lo

    first = core == 0
    p, q = jnp.where(first, x, y), jnp.where(first, y, x)

    def dev(dp=0, dz=0, dq=0, dc=0):
        pp, qq, zz = lax.rem(p + dp + 4, 4), lax.rem(q + dq + 4, 4), lax.rem(z + dz + 4, 4)
        xx, yy = jnp.where(first, pp, qq), jnp.where(first, qq, pp)
        cc = 1 - core if dc else core
        return ((lax.rem(xx, 2) * 4 + zz) * 2 + cc, yy * 2 + xx // 2)

    def reader(dc, dq):
        return dev(dp=dq, dc=1) if dc else dev(dq=dq)

    def remote(src, dst, send, recv, to):
        return pltpu.make_async_remote_copy(
            src_ref=src, dst_ref=dst, send_sem=send_sem.at[send], recv_sem=recv, device_id=to, device_id_type=MESH
        )

    proj_in = pltpu.make_async_copy(proj_hbm, proj_ref, in_sem.at[0])
    part_in = pltpu.make_async_copy(part_hbm, part_ref, in_sem.at[1])
    proj_in.start()
    part_in.start()
    plane = [(dx, dz) for dz in (2, 1, 3, 0) for dx in (2, 1, 3, 0) if (dx, dz) != (0, 0)]
    line = [(j, dc, dq) for j, (dc, dq) in enumerate(SLOTS) if j != OWN]
    near = [dev(dp=k) for k in (1, 2, 3)] + [dev(dz=k) for k in (1, 2, 3)] + [dev(dq=k) for k in (1, 2, 3)]
    near += [dev(dc=1)]
    barrier = pltpu.get_barrier_semaphore()
    for to in near:
        pl.semaphore_signal(barrier, inc=1, device_id=to, device_id_type=MESH)

    proj_in.wait()
    proj = proj_ref[...]
    inv_norm = lax.rsqrt(jnp.sum(proj * proj, axis=1, keepdims=True) + epsilon)
    inv[...] = jnp.broadcast_to(inv_norm, inv.shape)
    low = (proj * inv_norm).astype(BF16)
    u[0] = low
    rows[OWN] = low
    part_in.wait()

    enc[OWN] = part_ref[...].reshape(1, BLK)
    u32[COLS : COLS + 8, :] = jnp.zeros((8, PROJ), F32)
    acc[...] = jnp.zeros_like(acc)

    pl.semaphore_wait(barrier, len(near))

    def wait_for(ref, sem):
        pltpu.make_async_copy(ref, ref, sem).wait()

    def piece(s, half):
        return u.at[s, pl.ds(half * CUT, BLK - CUT if half else CUT), :]

    def along(half, d):
        return (d, 0) if half == 0 else (0, d)

    def push(s, half, axis, d):
        dx, dz = ORDER[s]
        t = STEP[((dx + d) % 4, dz) if axis == 0 else (dx, (dz + d) % 4)]
        remote(piece(s, half), piece(t, half), S_PLANE, own_sem.at[t, half], dev(dp=d) if axis == 0 else dev(dz=d)).start()

    def wait_half(s, half):
        wait_for(piece(s, half), own_sem.at[s, half])

    for half in (0, 1):
        for d in (1, 3):
            push(0, half, half, d)
    for half in (0, 1):
        push(0, half, half, 2)
    for dc, dq in ((0, 1), (0, 3), (0, 2), (1, 0)):
        remote(u.at[0], rows.at[SLOTS.index((dc, dq))], S_ROW, row_sem, reader(dc, dq)).start()
    for half in (1, 0):
        for d in (1, 3, 2):
            push(0, half, 1 - half, d)
    for d in (1, 3, 2):
        for half in (0, 1):
            s = STEP[along(half, d)]
            wait_half(s, half)
            for f in (1, 3, 2):
                push(s, half, 1 - half, f)
    for d in (1, 3, 2):
        s = STEP[(d, 0)]
        wait_half(s, 1)
        remote(u.at[s], rows.at[SLOTS.index((1, d))], S_ROW, row_sem, dev(dc=1)).start()
    for j, dc, dq in line:
        remote(enc.at[OWN], enc.at[j], S_ENC, enc_sem, reader(dc, dq)).start()
    wait_for(rows.at[pl.ds(0, 7)], row_sem)

    scale = inverse_temp * LOG2E
    r_iota = lax.broadcasted_iota(jnp.int32, (BLK, BLK), 0)
    c_iota = lax.broadcasted_iota(jnp.int32, (BLK, BLK), 1)

    def arrive(i):
        @pl.when((i >= 7) | ((i > 0) & (lax.rem(i, 2) == 0)))
        def _():
            wait_half(i, 0)

        @pl.when(i >= 7)
        def _():
            wait_half(i, 1)

    def compute(blocks):
        for i in blocks:
            arrive(i)
        for i in blocks:
            block = u[i]
            u32[pl.ds(pl.multiple_of(i * BLK, BLK), BLK), :] = block.astype(F32)
            for j in range(LINE):
                dots = lax.dot_general(rows[j], block, (((1,), (1,)), ((), ())), preferred_element_type=F32)
                ex = jnp.exp2(dots * scale)
                if j == OWN:
                    ex = jnp.where(r_iota == c_iota + i * BLK, 0.0, ex)
                acc[j] += ex[:, :128] + ex[:, 128:]
                e[j, i] = ex.astype(BF16)

    def two(n, carry):
        compute((2 * n, 2 * n + 1))
        return carry

    lax.fori_loop(0, PLANE // 2, two, 0)

    for j, (dc, dq) in enumerate(SLOTS):
        rs_send[j] = transposed_sum(acc[j])
        if j != OWN:
            remote(rs_send.at[j], rs_recv.at[j], S_RS, rs_sem, dev(dq=-dq, dc=dc)).start()

    wait_for(enc.at[pl.ds(0, 7)], enc_sem)
    v = enc[...]
    off, v_group, v_loop = v & 255, (v >> 8) & 7, v >> 11
    v_x, v_y = ((v_group & 1) << 1) + (v_loop >> 3), v_group >> 1
    v_p, v_q = jnp.where(first, v_x, v_y), jnp.where(first, v_y, v_x)
    key = ((p - v_p) & 3) * 4 + ((z - (v_loop >> 1)) & 3)
    place = jnp.zeros_like(v)
    for d, t in STEP.items():
        place = jnp.where(key == d[0] * 4 + d[1], t, place)
    index[...] = jnp.where(((v_loop & 1) == core) & (v_q == q), place * BLK + off, COLS)
    to_smem = pltpu.make_async_copy(index, index_s, local_sem)
    to_smem.start()
    to_smem.wait()

    def fetch(j, carry):
        for t in range(BLK):
            pick[j, t : t + 1, :] = u32[pl.ds(index_s[j, 0, t], 1), :]
        return carry

    lax.fori_loop(0, FIRST, fetch, 0)

    wait_for(rs_recv.at[pl.ds(0, 7)], rs_sem)
    row_sums = rs_send[OWN]
    for j, dc, dq in line:
        row_sums += rs_recv[j]
    recip = 1.0 / row_sums
    r_cols[0] = recip
    r_rows[OWN] = recip
    for dx, dz in plane:
        remote(r_cols.at[0], r_cols.at[STEP[(dx, dz)]], S_RCOL, rcol_sem, dev(dx, dz)).start()
    for j, dc, dq in line:
        remote(r_cols.at[0], r_rows.at[j], S_RROW, rrow_sem, reader(dc, dq)).start()

    lax.fori_loop(FIRST, LINE, fetch, 0)
    for j in range(LINE):
        both = rows[j].astype(F32) * pick[j]
        pos_send[j] = transposed_sum(both[:, :128] + both[:, 128:]) * inverse_temp
    for j, dc, dq in line:
        remote(pos_send.at[j], pos_recv.at[j], S_POS, pos_sem, dev(dq=-dq, dc=dc)).start()

    wait_for(r_rows.at[pl.ds(0, 7)], rrow_sem)
    for j in range(LINE):
        r = r_rows[j]
        for h in (0, 1):
            part = jnp.broadcast_to(r[:, h * 128 : (h + 1) * 128], (128, 128))
            ri[j, h * 128 : (h + 1) * 128, :] = jnp.transpose(part)
    wait_for(r_cols.at[pl.ds(1, PLANE - 1)], rcol_sem)

    def weigh(j, carry):
        r_row = jnp.concatenate([ri[j], ri[j]], axis=1)
        total = jnp.zeros((BLK, PROJ), F32)
        for pos in range(PLANE):
            w = e[j, pos].astype(F32) * (r_row + r_cols[pos])
            total += jnp.dot(w.astype(BF16), u[pos], preferred_element_type=F32)
        g_own[...] = inverse_temp * (total - 2.0 * pick[j])
        g_send[j] = g_own[...].astype(BF16)
        for t, dc, dq in line:

            @pl.when(j == t)
            def _():
                remote(g_send.at[t], g_recv.at[t], S_G, g_sem.at[t], dev(dq=-dq, dc=dc)).start()

        return carry

    lax.fori_loop(0, LINE, weigh, 0)

    wait_for(pos_recv.at[pl.ds(0, 7)], pos_sem)
    positive = pos_send[OWN]
    for j, dc, dq in line:
        positive += pos_recv[j]
    loss_ref[...] = (jnp.log(row_sums) - positive).reshape(BLK)
    for j in (6, 0, 1, 2, 3, 4, 5):
        wait_for(g_recv.at[j], g_sem.at[j])
        g_own[...] += g_recv[j].astype(F32)
    grad_unit = g_own[...]
    inv_b = jnp.concatenate([inv[...], inv[...]], axis=1)
    unit = proj_ref[...] * inv_b
    along = jnp.sum(unit * grad_unit, axis=1, keepdims=True)
    grad_ref[...] = inv_b * (grad_unit - unit * along)

    for sem, ref, n in (
        (S_PLANE, u, 15), (S_ROW, rows, 7), (S_ENC, enc, 7), (S_RS, rs_send, 7), (S_RCOL, r_cols, 15), (S_RROW, r_rows, 7),
        (S_POS, pos_send, 7), (S_G, g_send, 7),
    ):
        wait_for(ref.at[pl.ds(0, n)], send_sem.at[sem])


def on_device(projections, partners):
    dma = pltpu.SemaphoreType.DMA
    vmem = pl.BlockSpec(memory_space=pltpu.VMEM)
    loss, grad = pl.pallas_call(
        kernel,
        out_shape=(jax.ShapeDtypeStruct((BLK,), F32), jax.ShapeDtypeStruct((BLK, PROJ), F32)),
        in_specs=[pl.BlockSpec(memory_space=pltpu.HBM)] * 2,
        out_specs=(vmem, vmem),
        scratch_shapes=[
            pltpu.VMEM((BLK, PROJ), F32),
            pltpu.VMEM((BLK,), jnp.int32),
            pltpu.VMEM((PLANE, BLK, PROJ), BF16),
            pltpu.VMEM((COLS + 8, PROJ), F32),
            pltpu.VMEM((LINE, BLK, PROJ), BF16),
            pltpu.VMEM((LINE, PLANE, BLK, BLK), BF16),
            pltpu.VMEM((LINE, BLK, 128), F32),
            pltpu.VMEM((BLK, 128), F32),
            pltpu.VMEM((LINE, 1, BLK), jnp.int32),
            pltpu.VMEM((LINE, 1, BLK), jnp.int32),
            pltpu.SMEM((LINE, 1, BLK), jnp.int32),
            pltpu.VMEM((LINE, BLK, PROJ), F32),
            pltpu.VMEM((LINE, 1, BLK), F32),
            pltpu.VMEM((LINE, 1, BLK), F32),
            pltpu.VMEM((PLANE, 1, BLK), F32),
            pltpu.VMEM((LINE, 1, BLK), F32),
            pltpu.VMEM((LINE, BLK, 128), F32),
            pltpu.VMEM((LINE, 1, BLK), F32),
            pltpu.VMEM((LINE, 1, BLK), F32),
            pltpu.VMEM((BLK, PROJ), F32),
            pltpu.VMEM((LINE, BLK, PROJ), BF16),
            pltpu.VMEM((LINE, BLK, PROJ), BF16),
            dma((16, 2)), dma, dma, dma, dma, dma, dma, dma((7,)), dma((8,)), dma, dma((2,)),
        ],
        compiler_params=pltpu.CompilerParams(
            collective_id=0, has_side_effects=True, vmem_limit_bytes=54850 * 1024
        ),
        cost_estimate=pl.CostEstimate(flops=4 * LINE * BLK * COLS * PROJ, bytes_accessed=8 << 20, transcendentals=LINE * BLK * COLS),
    )(projections, partners)
    return loss, grad


def solution(mesh):
    return jax.shard_map(
        on_device,
        mesh=mesh,
        in_specs=(P(("loop", "group"), None), P(("loop", "group"))),
        out_specs=(P(("loop", "group")), P(("loop", "group"), None)),
        check_vma=False,
    )
```

```python
import jax
import jax.numpy as jnp
from jax import lax
from jax.experimental import pallas as pl
from jax.experimental.pallas import tpu as pltpu
from jax.sharding import PartitionSpec as P

MESH = pl.DeviceIdType.MESH
F32, BF16 = jnp.float32, jnp.bfloat16
epsilon = 1e-06
inverse_temp = 10.0
LOG2E = 1.4426950408889634

PROJ = 256
BLK = 256
RING = 4
PLANE = RING * RING
COLS = PLANE * BLK
LINE = 2 * RING

ORDER = [
    (0, 0), (1, 0), (0, 1), (3, 0), (0, 3), (2, 0), (0, 2), (1, 1),
    (3, 1), (1, 3), (3, 3), (1, 2), (3, 2), (2, 1), (2, 3), (2, 2),
]
STEP = {d: s for s, d in enumerate(ORDER)}
SLOTS = ((1, 2), (0, 2), (1, 1), (0, 1), (1, 3), (0, 3), (1, 0), (0, 0))
OWN = 7
CUT = 112
FIRST = 3
S_PLANE, S_ROW, S_ENC, S_RS, S_RCOL, S_RROW, S_POS, S_G = range(8)


def transposed_sum(v):
    parts = [jnp.sum(jnp.transpose(v[i * 128 : (i + 1) * 128, :]), axis=0, keepdims=True) for i in range(2)]
    return jnp.concatenate(parts, axis=1)


def kernel(
    proj_hbm, part_hbm, loss_ref, grad_ref,
    proj_ref, part_ref, u, u32, rows, e, acc, inv, enc, index, index_s, pick,
    rs_send, rs_recv, r_cols, r_rows, ri, pos_send, pos_recv, g_own, g_send, g_recv,
    own_sem, row_sem, enc_sem, rs_sem, rcol_sem, rrow_sem, pos_sem, g_sem, send_sem, local_sem, in_sem,
):
    loop, group = lax.axis_index("loop"), lax.axis_index("group")
    core, z, x_lo = lax.rem(loop, 2), lax.rem(loop // 2, 4), loop // 8
    y, x_hi = group // 2, lax.rem(group, 2)
    x = x_hi * 2 + x_lo

    first = core == 0
    p, q = jnp.where(first, x, y), jnp.where(first, y, x)

    def dev(dp=0, dz=0, dq=0, dc=0):
        pp, qq, zz = lax.rem(p + dp + 4, 4), lax.rem(q + dq + 4, 4), lax.rem(z + dz + 4, 4)
        xx, yy = jnp.where(first, pp, qq), jnp.where(first, qq, pp)
        cc = 1 - core if dc else core
        return ((lax.rem(xx, 2) * 4 + zz) * 2 + cc, yy * 2 + xx // 2)

    def reader(dc, dq):
        return dev(dp=dq, dc=1) if dc else dev(dq=dq)

    def remote(src, dst, send, recv, to):
        return pltpu.make_async_remote_copy(
            src_ref=src, dst_ref=dst, send_sem=send_sem.at[send], recv_sem=recv, device_id=to, device_id_type=MESH
        )

    proj_in = pltpu.make_async_copy(proj_hbm, proj_ref, in_sem.at[0])
    part_in = pltpu.make_async_copy(part_hbm, part_ref, in_sem.at[1])
    proj_in.start()
    part_in.start()
    plane = [(dx, dz) for dz in (2, 1, 3, 0) for dx in (2, 1, 3, 0) if (dx, dz) != (0, 0)]
    line = [(j, dc, dq) for j, (dc, dq) in enumerate(SLOTS) if j != OWN]
    near = [dev(dp=k) for k in (1, 2, 3)] + [dev(dz=k) for k in (1, 2, 3)] + [dev(dq=k) for k in (1, 2, 3)]
    near += [dev(dc=1)]
    barrier = pltpu.get_barrier_semaphore()
    for to in near:
        pl.semaphore_signal(barrier, inc=1, device_id=to, device_id_type=MESH)

    proj_in.wait()
    proj = proj_ref[...]
    inv_norm = lax.rsqrt(jnp.sum(proj * proj, axis=1, keepdims=True) + epsilon)
    inv[...] = jnp.broadcast_to(inv_norm, inv.shape)
    low = (proj * inv_norm).astype(BF16)
    u[0] = low
    rows[OWN] = low
    part_in.wait()

    enc[OWN] = part_ref[...].reshape(1, BLK)
    u32[COLS : COLS + 8, :] = jnp.zeros((8, PROJ), F32)
    acc[...] = jnp.zeros_like(acc)

    pl.semaphore_wait(barrier, len(near))

    def wait_for(ref, sem):
        pltpu.make_async_copy(ref, ref, sem).wait()

    def piece(s, half):
        return u.at[s, pl.ds(half * CUT, BLK - CUT if half else CUT), :]

    def along(half, d):
        return (d, 0) if half == 0 else (0, d)

    def push(s, half, axis, d):
        dx, dz = ORDER[s]
        t = STEP[((dx + d) % 4, dz) if axis == 0 else (dx, (dz + d) % 4)]
        remote(piece(s, half), piece(t, half), S_PLANE, own_sem.at[t, half], dev(dp=d) if axis == 0 else dev(dz=d)).start()

    def wait_half(s, half):
        wait_for(piece(s, half), own_sem.at[s, half])

    for half in (0, 1):
        for d in (1, 3):
            push(0, half, half, d)
    for half in (0, 1):
        push(0, half, half, 2)
    for dc, dq in ((0, 1), (0, 3), (0, 2), (1, 0)):
        remote(u.at[0], rows.at[SLOTS.index((dc, dq))], S_ROW, row_sem, reader(dc, dq)).start()
    for half in (1, 0):
        for d in (1, 3, 2):
            push(0, half, 1 - half, d)
    for d in (1, 3, 2):
        for half in (0, 1):
            s = STEP[along(half, d)]
            wait_half(s, half)
            for f in (1, 3, 2):
                push(s, half, 1 - half, f)
    for d in (1, 3, 2):
        s = STEP[(d, 0)]
        wait_half(s, 1)
        remote(u.at[s], rows.at[SLOTS.index((1, d))], S_ROW, row_sem, dev(dc=1)).start()
    for j, dc, dq in line:
        remote(enc.at[OWN], enc.at[j], S_ENC, enc_sem, reader(dc, dq)).start()
    wait_for(rows.at[pl.ds(0, 7)], row_sem)

    scale = inverse_temp * LOG2E
    r_iota = lax.broadcasted_iota(jnp.int32, (BLK, BLK), 0)
    c_iota = lax.broadcasted_iota(jnp.int32, (BLK, BLK), 1)

    def arrive(i):
        @pl.when((i >= 7) | ((i > 0) & (lax.rem(i, 2) == 0)))
        def _():
            wait_half(i, 0)

        @pl.when(i >= 7)
        def _():
            wait_half(i, 1)

    def compute(blocks):
        for i in blocks:
            arrive(i)
        for i in blocks:
            block = u[i]
            u32[pl.ds(pl.multiple_of(i * BLK, BLK), BLK), :] = block.astype(F32)
            for j in range(LINE):
                dots = lax.dot_general(rows[j], block, (((1,), (1,)), ((), ())), preferred_element_type=F32)
                ex = jnp.exp2(dots * scale)
                if j == OWN:
                    ex = jnp.where(r_iota == c_iota + i * BLK, 0.0, ex)
                acc[j] += ex[:, :128] + ex[:, 128:]
                e[j, i] = ex.astype(BF16)

    def two(n, carry):
        compute((2 * n, 2 * n + 1))
        return carry

    compute((0, 1, 2, 3))
    lax.fori_loop(2, PLANE // 2, two, 0)

    for j, (dc, dq) in enumerate(SLOTS):
        rs_send[j] = transposed_sum(acc[j])
        if j != OWN:
            remote(rs_send.at[j], rs_recv.at[j], S_RS, rs_sem, dev(dq=-dq, dc=dc)).start()

    wait_for(enc.at[pl.ds(0, 7)], enc_sem)
    v = enc[...]
    off, v_group, v_loop = v & 255, (v >> 8) & 7, v >> 11
    v_x, v_y = ((v_group & 1) << 1) + (v_loop >> 3), v_group >> 1
    v_p, v_q = jnp.where(first, v_x, v_y), jnp.where(first, v_y, v_x)
    key = ((p - v_p) & 3) * 4 + ((z - (v_loop >> 1)) & 3)
    place = jnp.zeros_like(v)
    for d, t in STEP.items():
        place = jnp.where(key == d[0] * 4 + d[1], t, place)
    index[...] = jnp.where(((v_loop & 1) == core) & (v_q == q), place * BLK + off, COLS)
    to_smem = pltpu.make_async_copy(index, index_s, local_sem)
    to_smem.start()
    to_smem.wait()

    def fetch(j, carry):
        for t in range(BLK):
            pick[j, t : t + 1, :] = u32[pl.ds(index_s[j, 0, t], 1), :]
        return carry

    lax.fori_loop(0, FIRST, fetch, 0)

    wait_for(rs_recv.at[pl.ds(0, 7)], rs_sem)
    row_sums = rs_send[OWN]
    for j, dc, dq in line:
        row_sums += rs_recv[j]
    recip = 1.0 / row_sums
    r_cols[0] = recip
    r_rows[OWN] = recip
    for dx, dz in plane:
        remote(r_cols.at[0], r_cols.at[STEP[(dx, dz)]], S_RCOL, rcol_sem, dev(dx, dz)).start()
    for j, dc, dq in line:
        remote(r_cols.at[0], r_rows.at[j], S_RROW, rrow_sem, reader(dc, dq)).start()

    lax.fori_loop(FIRST, LINE, fetch, 0)
    for j in range(LINE):
        both = rows[j].astype(F32) * pick[j]
        pos_send[j] = transposed_sum(both[:, :128] + both[:, 128:]) * inverse_temp
    for j, dc, dq in line:
        remote(pos_send.at[j], pos_recv.at[j], S_POS, pos_sem, dev(dq=-dq, dc=dc)).start()

    wait_for(r_rows.at[pl.ds(0, 7)], rrow_sem)
    for j in range(LINE):
        r = r_rows[j]
        for h in (0, 1):
            part = jnp.broadcast_to(r[:, h * 128 : (h + 1) * 128], (128, 128))
            ri[j, h * 128 : (h + 1) * 128, :] = jnp.transpose(part)
    wait_for(r_cols.at[pl.ds(1, PLANE - 1)], rcol_sem)

    def weigh(j, carry):
        r_row = jnp.concatenate([ri[j], ri[j]], axis=1)
        total = jnp.zeros((BLK, PROJ), F32)
        for pos in range(PLANE):
            w = e[j, pos].astype(F32) * (r_row + r_cols[pos])
            total += jnp.dot(w.astype(BF16), u[pos], preferred_element_type=F32)
        g_own[...] = inverse_temp * (total - 2.0 * pick[j])
        g_send[j] = g_own[...].astype(BF16)
        for t, dc, dq in line:

            @pl.when(j == t)
            def _():
                remote(g_send.at[t], g_recv.at[t], S_G, g_sem.at[t], dev(dq=-dq, dc=dc)).start()

        return carry

    lax.fori_loop(0, LINE, weigh, 0)

    wait_for(pos_recv.at[pl.ds(0, 7)], pos_sem)
    positive = pos_send[OWN]
    for j, dc, dq in line:
        positive += pos_recv[j]
    loss_ref[...] = (jnp.log(row_sums) - positive).reshape(BLK)
    for j in (6, 0, 1, 2, 3, 4, 5):
        wait_for(g_recv.at[j], g_sem.at[j])
        g_own[...] += g_recv[j].astype(F32)
    grad_unit = g_own[...]
    inv_b = jnp.concatenate([inv[...], inv[...]], axis=1)
    unit = proj_ref[...] * inv_b
    along = jnp.sum(unit * grad_unit, axis=1, keepdims=True)
    grad_ref[...] = inv_b * (grad_unit - unit * along)

    for sem, ref, n in (
        (S_PLANE, u, 15), (S_ROW, rows, 7), (S_ENC, enc, 7), (S_RS, rs_send, 7), (S_RCOL, r_cols, 15), (S_RROW, r_rows, 7),
        (S_POS, pos_send, 7), (S_G, g_send, 7),
    ):
        wait_for(ref.at[pl.ds(0, n)], send_sem.at[sem])


def on_device(projections, partners):
    dma = pltpu.SemaphoreType.DMA
    vmem = pl.BlockSpec(memory_space=pltpu.VMEM)
    loss, grad = pl.pallas_call(
        kernel,
        out_shape=(jax.ShapeDtypeStruct((BLK,), F32), jax.ShapeDtypeStruct((BLK, PROJ), F32)),
        in_specs=[pl.BlockSpec(memory_space=pltpu.HBM)] * 2,
        out_specs=(vmem, vmem),
        scratch_shapes=[
            pltpu.VMEM((BLK, PROJ), F32),
            pltpu.VMEM((BLK,), jnp.int32),
            pltpu.VMEM((PLANE, BLK, PROJ), BF16),
            pltpu.VMEM((COLS + 8, PROJ), F32),
            pltpu.VMEM((LINE, BLK, PROJ), BF16),
            pltpu.VMEM((LINE, PLANE, BLK, BLK), BF16),
            pltpu.VMEM((LINE, BLK, 128), F32),
            pltpu.VMEM((BLK, 128), F32),
            pltpu.VMEM((LINE, 1, BLK), jnp.int32),
            pltpu.VMEM((LINE, 1, BLK), jnp.int32),
            pltpu.SMEM((LINE, 1, BLK), jnp.int32),
            pltpu.VMEM((LINE, BLK, PROJ), F32),
            pltpu.VMEM((LINE, 1, BLK), F32),
            pltpu.VMEM((LINE, 1, BLK), F32),
            pltpu.VMEM((PLANE, 1, BLK), F32),
            pltpu.VMEM((LINE, 1, BLK), F32),
            pltpu.VMEM((LINE, BLK, 128), F32),
            pltpu.VMEM((LINE, 1, BLK), F32),
            pltpu.VMEM((LINE, 1, BLK), F32),
            pltpu.VMEM((BLK, PROJ), F32),
            pltpu.VMEM((LINE, BLK, PROJ), BF16),
            pltpu.VMEM((LINE, BLK, PROJ), BF16),
            dma((16, 2)), dma, dma, dma, dma, dma, dma, dma((7,)), dma((8,)), dma, dma((2,)),
        ],
        compiler_params=pltpu.CompilerParams(
            collective_id=0, has_side_effects=True, vmem_limit_bytes=54850 * 1024
        ),
        cost_estimate=pl.CostEstimate(flops=4 * LINE * BLK * COLS * PROJ, bytes_accessed=8 << 20, transcendentals=LINE * BLK * COLS),
    )(projections, partners)
    return loss, grad


def solution(mesh):
    return jax.shard_map(
        on_device,
        mesh=mesh,
        in_specs=(P(("loop", "group"), None), P(("loop", "group"))),
        out_specs=(P(("loop", "group")), P(("loop", "group"), None)),
        check_vma=False,
    )
```
